256 devices in a mesh: row: 8 (over y, core), col: 32 (over x, z).
Axes of the slice: x: 4, y: 4, z: 8, core: 2. Of those that a mesh axis runs over, the one named last changes fastest.
Arguments:
- outside: bfloat16 [4096, 16384], P('row', 'col'), may hold values from 0.0099 to 17.5
- inside_head: bfloat16 [4096, 16384], P('row', 'col'), may hold values from 0.0099 to 17.5
- inside_tail: bfloat16 [4096, 16384], P('row', 'col'), may hold values from 0.0099 to 17.5
- inside_pair: float32 [512, 16384], P(None, 'col'), may hold values from 0.4 to 1.6
- seq_head: int32 [1, 16384], P(None, 'col'), may hold values from 0 to 3
- seq_tail: int32 [1, 16384], P(None, 'col'), may hold values from 0 to 3
- pair_mask: int32 [4, 128], P(None, 'col'), may hold values 0 or 1
- split_weight: float32 [4], replicated, may hold values from 0.5 to 2
- pair_weight: float32 [4, 4], replicated, may hold values from 0.5 to 2
- span_blocks: int32 [1], replicated, may hold values from 32 to 255
- partition: float32 [1], replicated, may hold values from 1 to 3
Outputs:
- outside_out: float32 [4096, 16384], P('row', 'col')
- prob_out: float32 [4096, 16384], P('row', 'col')
The draws below stay inside these ranges and needn't reach their ends.
All inputs are finite; a program needn't handle non-finite values. No bound on the sum of `pair_mask` on one device may be relied on, other than what follows from the above.
Results may differ from the reference program's by a relative error of at most 0.0003.
Values may be sent and summed in bfloat16 or wider, within the bound.
A program may use at most 64 MiB of HBM per device.

```python
import math
import jax
import jax.numpy as jnp
from jax import lax

BLK = 512
CYC = 1
SUB = 4
BAND_ROWS = 4096
END_NT = 16384
N_ROW = 8
N_COL = 32


def spiked_table(key):
    tile_rows = BAND_ROWS // BLK
    tile_cols = END_NT // BLK
    key_back, key_order, key_height = jax.random.split(key, 3)
    background = jnp.exp(jax.random.uniform(key_back, (BAND_ROWS, END_NT), jnp.float32, jnp.log(0.01), jnp.log(0.2)))
    order_keys = jax.random.split(key_order, tile_rows * tile_cols)
    orders = jax.vmap(lambda subkey: jax.random.permutation(subkey, BLK))(order_keys).reshape(tile_rows, tile_cols, BLK)
    spiked = orders[:, :, :, None] == jnp.arange(BLK, dtype=jnp.int32)[None, None, None, :]
    spiked = spiked.transpose(0, 2, 1, 3).reshape(BAND_ROWS, END_NT)
    height = jax.random.uniform(key_height, (BAND_ROWS, END_NT), jnp.float32, 16.5, 17.5)
    return jnp.where(spiked, height, background).astype(jnp.bfloat16)


def draw_outside(key, part):
    return spiked_table(jax.random.fold_in(key, 101))


def draw_inside_head(key, part):
    return spiked_table(jax.random.fold_in(key, 202))


def draw_inside_tail(key, part):
    return spiked_table(jax.random.fold_in(key, 303))


def place_ends(result, stream_key, low, high):
    longest = result.shape.index(max(result.shape))
    spots = []
    for shift in (0, 1):
        where = [jax.random.randint(jax.random.fold_in(stream_key, axis), (), 0, length) for axis, length in enumerate(result.shape)]
        where[longest] = (where[longest] + shift) % result.shape[longest]
        spots.append(tuple(where))
    return result.at[spots[0]].set(low).at[spots[1]].set(high)


def steps_of(key, extent, cuts, least, top_value):
    def one(axis_at, parts):
        draws = jax.random.uniform(jax.random.fold_in(jax.random.fold_in(key, 6), axis_at), (parts,), jnp.float32, least / len(cuts), top_value / len(cuts))
        return jnp.repeat(jnp.exp(draws), extent[axis_at] // parts).reshape((-1,) + (1,) * (len(extent) - axis_at - 1))

    gain = one(*cuts[0])
    for cut in cuts[1:]:
        gain = gain * one(*cut)
    return gain


def setup_inputs(seed: int = 0) -> dict:
    seeds = jax.random.split(jax.random.key(seed), 12)
    return {
        "outside": draw_outside(jax.random.fold_in(seeds[11], 71), 0),
        "inside_head": draw_inside_head(jax.random.fold_in(seeds[11], 71), 0),
        "inside_tail": draw_inside_tail(jax.random.fold_in(seeds[11], 71), 0),
        "inside_pair": jnp.clip(jnp.exp(math.log(1.6) - 1.3862944 * jax.random.uniform(seeds[3], (CYC * BLK, END_NT), jnp.float32) ** steps_of(seeds[3], (CYC * BLK, END_NT), ((1, 32),), -0.2, 0.2)), 0.4, 1.6),
        "seq_head": place_ends(jax.random.randint(seeds[4], (CYC, END_NT), 0, 4), jax.random.fold_in(seeds[4], 1), 0, 3).astype(jnp.int32),
        "seq_tail": place_ends(jax.random.randint(seeds[5], (CYC, END_NT), 0, 4), jax.random.fold_in(seeds[5], 1), 0, 3).astype(jnp.int32),
        "pair_mask": place_ends((jax.random.randint(seeds[6], (CYC * SUB, N_COL * SUB), 0, 4) < 3).astype(jnp.int32), jax.random.fold_in(seeds[6], 1), 0, 1),
        "split_weight": jnp.clip(jnp.exp(jax.random.uniform(seeds[7], (4,), jnp.float32, math.log(0.5), math.log(2.0))), 0.5, 2.0),
        "pair_weight": jnp.clip(jnp.exp(jax.random.uniform(seeds[8], (4, 4), jnp.float32, math.log(0.5), math.log(2.0))), 0.5, 2.0),
        "span_blocks": jax.random.randint(seeds[9], (1,), N_COL, 8 * N_COL).astype(jnp.int32),
        "partition": jnp.clip(jnp.exp(jax.random.uniform(seeds[10], (1,), jnp.float32, math.log(1.0), math.log(3.0))), 1.0, 3.0),
    }


precise = lax.Precision.HIGHEST

def finish(right_sum, left_sum, head_codes, tail_codes, mask_rows, pair_rows, split_weight, pair_weight, span_blocks, partition, owner_factor):
    cycles, tile_size = head_codes.shape
    repeat = tile_size // mask_rows.shape[1]
    allowed = jnp.repeat(jnp.repeat(mask_rows.astype(jnp.float32), repeat, axis=0), repeat, axis=1).reshape(cycles, tile_size, tile_size)
    letters = jnp.arange(4, dtype=jnp.int32)
    head_hot = (head_codes[:, :, None] == letters[None, None, :]).astype(jnp.float32)
    tail_hot = (tail_codes[:, :, None] == letters[None, None, :]).astype(jnp.float32)
    head_weight = jnp.einsum('mak,k->ma', head_hot, split_weight, precision=precise)
    tail_weight = jnp.einsum('mak,k->ma', tail_hot, split_weight, precision=precise)
    outside_diag = owner_factor * allowed * (right_sum * tail_weight[:, None, :] + head_weight[:, :, None] * left_sum) / tile_size
    pair_table = jnp.einsum('mak,kl,mbl->mab', head_hot, pair_weight, tail_hot, precision=precise)
    positions = jnp.arange(tile_size, dtype=jnp.float32)
    span_nt = tile_size * span_blocks[0].astype(jnp.float32) + positions[None, :] - positions[:, None]
    penalty = jnp.sqrt(64.0 * tile_size / span_nt)
    pair_prob = pair_rows.reshape(cycles, tile_size, tile_size) * outside_diag * pair_table * penalty[None, :, :] / partition[0]
    return (outside_diag.reshape(cycles * tile_size, tile_size), pair_prob.reshape(cycles * tile_size, tile_size))

def row_tiles(array, row_index):
    block = array[row_index * CYC * BLK:(row_index + 1) * CYC * BLK]
    return block.reshape(CYC, BLK, N_COL, BLK).transpose(2, 0, 1, 3).astype(jnp.float32)

def reference(outside, inside_head, inside_tail, inside_pair, seq_head, seq_tail, pair_mask, split_weight, pair_weight, span_blocks, partition):
    col_ids = jnp.arange(N_COL, dtype=jnp.int32)
    right_all = jnp.zeros((N_COL, CYC, BLK, BLK), jnp.float32)
    left_all = jnp.zeros((N_COL, CYC, BLK, BLK), jnp.float32)
    for row_index in range(N_ROW):
        out_tiles = row_tiles(outside, row_index)
        head_tiles = row_tiles(inside_head, row_index)
        tail_tiles = row_tiles(inside_tail, row_index)
        right_term = jnp.einsum('jmac,jmbc->jmab', out_tiles, tail_tiles, precision=precise)
        left_term = jnp.einsum('jmca,jmcb->jmab', head_tiles, out_tiles, precision=precise)
        reach = (col_ids - row_index) % N_ROW
        reach = jnp.where(reach == 0, N_ROW, reach)
        earlier = jnp.concatenate([jnp.zeros_like(left_term[:, :1]), left_term[:, :-1]], axis=1)
        left_all = left_all + jnp.where((col_ids < reach)[:, None, None, None], earlier, left_term)
        window = jnp.zeros_like(right_term)
        for distance in range(1, N_ROW + 1):
            window = window + jnp.roll(right_term, -distance, axis=0)
        right_all = jnp.where((col_ids % N_ROW == row_index)[:, None, None, None], window, right_all)
    outside_out = jnp.zeros(outside.shape, jnp.float32)
    prob_out = jnp.zeros(outside.shape, jnp.float32)
    for col_index in range(N_COL):
        owner_row = col_index % N_ROW
        diag_rows, prob_rows = finish(right_all[col_index], left_all[col_index], seq_head[:, col_index * BLK:(col_index + 1) * BLK], seq_tail[:, col_index * BLK:(col_index + 1) * BLK], pair_mask[:, col_index * SUB:(col_index + 1) * SUB], inside_pair[:, col_index * BLK:(col_index + 1) * BLK], split_weight, pair_weight, span_blocks, partition, 1.0)
        outside_out = outside_out.at[owner_row * CYC * BLK:(owner_row + 1) * CYC * BLK, col_index * BLK:(col_index + 1) * BLK].set(diag_rows)
        prob_out = prob_out.at[owner_row * CYC * BLK:(owner_row + 1) * CYC * BLK, col_index * BLK:(col_index + 1) * BLK].set(prob_rows)
    return (outside_out, prob_out)
```

```python
import functools
import math

import jax
import jax.numpy as jnp
from jax import lax
from jax.experimental import pallas as pl
from jax.experimental.pallas import tpu as pltpu
from jax.sharding import PartitionSpec as P

MESH = pl.DeviceIdType.MESH
BLK = 512
ROWS = 8
COLS = 32
RIGHT_CHUNK = 32
RIGHT_CHUNKS = BLK // RIGHT_CHUNK
LEFT_CHUNK = 128
LEFT_CHUNKS = BLK // LEFT_CHUNK

LOG_LOW = math.log(BLK * 0.0099**2) - 0.01
LOG_HIGH = math.log(3 * BLK * 17.5**2) + 0.01
LOG_MIDDLE = (LOG_LOW + LOG_HIGH) / 2
LOG_STEP = (LOG_HIGH - LOG_LOW) / 65534


def encode(x):
    code = jnp.round((jnp.log(x) - LOG_MIDDLE) * (1.0 / LOG_STEP))
    return jnp.clip(code, -32767.0, 32767.0).astype(jnp.int32).astype(jnp.int16)


def decode(code):
    return jnp.exp(code.astype(jnp.int32).astype(jnp.float32) * LOG_STEP + LOG_MIDDLE)


def kernel(
    outside,
    inside_head,
    inside_tail,
    inside_pair,
    seq_head_any,
    seq_tail_any,
    pair_mask_any,
    split_weight_any,
    pair_weight_any,
    span_blocks_any,
    partition_any,
    outside_out,
    prob_out,
    out_tile,
    head_tile,
    tail_tile,
    factor,
    seq_head,
    seq_tail,
    pair_mask,
    split_weight,
    pair_weight,
    span_blocks,
    partition,
    right,
    left,
    right_code,
    left_code,
    right_in,
    left_in,
    load_sem,
    right_send,
    right_recv,
    left_send,
    left_recv,
):
    row = lax.axis_index("row")
    col = lax.axis_index("col")
    core = lax.rem(row, 2)
    along = lax.rem(col - 2 * (row // 2) + 32, 8)
    reach = lax.rem(col - row + 31, 8) + 1
    is_owner = reach == 8
    owner_row = lax.rem(col, 8)

    def at_col(c):
        return (row, lax.rem(c + COLS, COLS))

    def at_row(r):
        return (lax.rem(r + ROWS, ROWS), col)

    has_up = (along == 2) | (along == 3) | (along == 6) | (along == 7)
    passes_on = (along >= 3) & (along <= 6)
    next_col = jnp.where(passes_on, jnp.where(along <= 4, col - 1, col + 1), col - reach)
    next_slot = jnp.where(
        passes_on | (along == 2), 0, jnp.where(along == 7, 1, jnp.where(is_owner, 3, 2))
    )

    loads = [
        pltpu.make_async_copy(src, dst, load_sem.at[n])
        for n, (src, dst) in enumerate(
            ((outside, out_tile), (inside_tail, tail_tile), (inside_head, head_tile))
        )
    ]
    for load in loads:
        load.start()

    barrier = pltpu.get_barrier_semaphore()

    @pl.when(has_up)
    def _():
        up = jnp.where(along <= 3, col + 1, col - 1)
        pl.semaphore_signal(barrier, inc=1, device_id=at_col(up), device_id_type=MESH)

    @pl.when(is_owner)
    def _():
        for far in (2 - core, 7 - core, 1 + 6 * core, 8):
            pl.semaphore_signal(barrier, inc=1, device_id=at_col(col + far), device_id_type=MESH)
        for away in range(1, ROWS):
            pl.semaphore_signal(
                barrier, inc=1, device_id=at_row(row + away), device_id_type=MESH
            )

    loads[0].wait()
    loads[1].wait()

    def right_block(n, carry):
        rows = pl.ds(pl.multiple_of(n * 128, 128), 128)
        right[rows, :] = lax.dot_general(
            out_tile[rows, :],
            tail_tile[...],
            (((1,), (1,)), ((), ())),
            preferred_element_type=jnp.float32,
        )
        return carry

    lax.fori_loop(0, 4, right_block, 0)

    pl.semaphore_wait(barrier, jnp.where(is_owner, 1, 2))

    def right_copy(n):
        rows = pl.ds(pl.multiple_of(n * RIGHT_CHUNK, RIGHT_CHUNK), RIGHT_CHUNK)
        return pltpu.make_async_remote_copy(
            src_ref=right_code.at[rows],
            dst_ref=right_in.at[next_slot, rows],
            send_sem=right_send.at[n],
            recv_sem=right_recv.at[next_slot, n],
            device_id=at_col(next_col),
            device_id_type=MESH,
        )

    def right_arrival(slot, n):
        rows = pl.ds(pl.multiple_of(n * RIGHT_CHUNK, RIGHT_CHUNK), RIGHT_CHUNK)
        return pltpu.make_async_remote_copy(
            src_ref=right_code.at[rows],
            dst_ref=right_in.at[slot, rows],
            send_sem=right_send.at[n],
            recv_sem=right_recv.at[slot, n],
            device_id=at_col(next_col),
            device_id_type=MESH,
        )

    @pl.when(jnp.logical_not(has_up))
    def _():
        def step(n, carry):
            rows = pl.ds(pl.multiple_of(n * RIGHT_CHUNK, RIGHT_CHUNK), RIGHT_CHUNK)
            right_code[rows, :] = encode(right[rows, :])
            right_copy(n).start()
            return carry

        lax.fori_loop(0, RIGHT_CHUNKS, step, 0)

    loads[2].wait()

    def left_copy(n):
        rows = pl.ds(pl.multiple_of(n * LEFT_CHUNK, LEFT_CHUNK), LEFT_CHUNK)
        slot = lax.rem(row - owner_row + 7, 8)
        return pltpu.make_async_remote_copy(
            src_ref=left_code.at[rows],
            dst_ref=left_in.at[slot, rows],
            send_sem=left_send.at[n],
            recv_sem=left_recv.at[slot, n],
            device_id=at_row(owner_row),
            device_id_type=MESH,
        )

    for n in range(4):
        rows = slice(n * 128, n * 128 + 128)
        left[rows, :] = lax.dot_general(
            head_tile[:, rows],
            out_tile[...],
            (((0,), (0,)), ((), ())),
            preferred_element_type=jnp.float32,
        )

    @pl.when(jnp.logical_not(is_owner))
    def _():
        def step(n, carry):
            rows = pl.ds(pl.multiple_of(n * LEFT_CHUNK, LEFT_CHUNK), LEFT_CHUNK)
            left_code[rows, :] = encode(left[rows, :])
            left_copy(n).start()
            return carry

        lax.fori_loop(0, LEFT_CHUNKS, step, 0)

    @pl.when(has_up)
    def _():
        def step(n, carry):
            rows = pl.ds(pl.multiple_of(n * RIGHT_CHUNK, RIGHT_CHUNK), RIGHT_CHUNK)
            right_arrival(0, n).wait_recv()
            right_code[rows, :] = encode(right[rows, :] + decode(right_in[0, rows, :]))
            right_copy(n).start()
            return carry

        lax.fori_loop(0, RIGHT_CHUNKS, step, 0)

    @pl.when(jnp.logical_not(is_owner))
    def _():
        outside_out[...] = jnp.zeros((BLK, BLK), jnp.float32)
        prob_out[...] = jnp.zeros((BLK, BLK), jnp.float32)

    @pl.when(is_owner)
    def _():
        owner_loads = [
            pltpu.make_async_copy(src, dst, load_sem.at[3 + n])
            for n, (src, dst) in enumerate(
                (
                    (inside_pair, factor),
                    (seq_head_any, seq_head),
                    (seq_tail_any, seq_tail),
                    (pair_mask_any, pair_mask),
                    (split_weight_any, split_weight),
                    (pair_weight_any, pair_weight),
                    (span_blocks_any, span_blocks),
                    (partition_any, partition),
                )
            )
        ]
        for load in owner_loads:
            load.start()
        for load in owner_loads:
            load.wait()
        head_codes = jnp.transpose(
            jnp.broadcast_to(seq_head[...].astype(jnp.float32), (8, BLK)), (1, 0)
        )[:, :1]
        tail_codes = seq_tail[...]

        def chosen(codes, values):
            picked = jnp.where(codes == 1, values[1], values[0])
            picked = jnp.where(codes == 2, values[2], picked)
            return jnp.where(codes == 3, values[3], picked)

        weights = [split_weight[n] for n in range(4)]
        tail_weight = chosen(tail_codes, weights)
        pair_rows = [chosen(tail_codes, [pair_weight[h, t] for t in range(4)]) for h in range(4)]
        lane = lax.broadcasted_iota(jnp.int32, (1, BLK), 1)
        span_nt = BLK * span_blocks[0].astype(jnp.float32)

        blocks = [slice(n * 128, n * 128 + 128) for n in range(4)]
        for rows in blocks:
            codes = head_codes[rows]
            table = chosen(codes, pair_rows)
            place = lax.broadcasted_iota(jnp.int32, (128, BLK), 0) + rows.start
            across = lax.broadcasted_iota(jnp.int32, (128, BLK), 1)
            span = span_nt + (across - place).astype(jnp.float32)
            penalty = jnp.sqrt(64.0 * BLK / span)
            factor[rows, :] = factor[rows, :] * table * penalty / partition[0]

        def left_arrival(slot, n):
            rows = pl.ds(pl.multiple_of(n * LEFT_CHUNK, LEFT_CHUNK), LEFT_CHUNK)
            return pltpu.make_async_remote_copy(
                src_ref=left_code.at[rows],
                dst_ref=left_in.at[slot, rows],
                send_sem=left_send.at[n],
                recv_sem=left_recv.at[slot, n],
                device_id=at_row(owner_row + 1),
                device_id_type=MESH,
            )

        def counts(r):
            return col >= lax.rem(col - r + 31, 8) + 1

        def right_near(n, carry):
            rows = pl.ds(pl.multiple_of(n * RIGHT_CHUNK, RIGHT_CHUNK), RIGHT_CHUNK)
            right_arrival(2, n).wait_recv()
            right_arrival(3, n).wait_recv()
            right[rows, :] = decode(right_in[2, rows, :]) + decode(right_in[3, rows, :])
            return carry

        def left_add(n, carry):
            rows = pl.ds(pl.multiple_of(n * LEFT_CHUNK, LEFT_CHUNK), LEFT_CHUNK)
            total = jnp.where(counts(row), left[rows, :], 0.0)
            for slot in range(7):
                left_arrival(slot, n).wait_recv()
                total = total + jnp.where(
                    counts(lax.rem(row + slot + 1, ROWS)), decode(left_in[slot, rows, :]), 0.0
                )
            left[rows, :] = total
            return carry

        lax.fori_loop(0, RIGHT_CHUNKS, right_near, 0)
        lax.fori_loop(0, LEFT_CHUNKS, left_add, 0)

        for b, rows in enumerate(blocks):
            codes = head_codes[rows]
            head_weight = chosen(codes, weights)
            allowed = chosen(lane // 128, [pair_mask[b, n].astype(jnp.float32) for n in range(4)])
            for part in range(128 // RIGHT_CHUNK):
                n = b * (128 // RIGHT_CHUNK) + part
                here = slice(n * RIGHT_CHUNK, (n + 1) * RIGHT_CHUNK)
                inner = slice(part * RIGHT_CHUNK, (part + 1) * RIGHT_CHUNK)
                right_arrival(0, n).wait_recv()
                right_arrival(1, n).wait_recv()
                right_sum = right[here, :] + decode(right_in[0, here, :]) + decode(right_in[1, here, :])
                diag = (
                    allowed
                    * (right_sum * tail_weight + head_weight[inner] * left[here, :])
                    * (1.0 / BLK)
                )
                outside_out[here, :] = diag
                prob_out[here, :] = diag * factor[here, :]

    def sent(n, carry):
        right_copy(n).wait_send()
        return carry

    lax.fori_loop(0, RIGHT_CHUNKS, sent, 0)

    @pl.when(jnp.logical_not(is_owner))
    def _():
        for n in range(LEFT_CHUNKS):
            left_copy(n).wait_send()


def per_device(*args):
    vmem = pl.BlockSpec(memory_space=pltpu.VMEM)
    anywhere = pl.BlockSpec(memory_space=pl.ANY)
    tile = jax.ShapeDtypeStruct((BLK, BLK), jnp.float32)
    return pl.pallas_call(
        kernel,
        out_shape=(tile, tile),
        in_specs=[anywhere] * 11,
        out_specs=(vmem, vmem),
        scratch_shapes=[
            pltpu.VMEM((BLK, BLK), jnp.bfloat16),
            pltpu.VMEM((BLK, BLK), jnp.bfloat16),
            pltpu.VMEM((BLK, BLK), jnp.bfloat16),
            pltpu.VMEM((BLK, BLK), jnp.float32),
            pltpu.VMEM((1, BLK), jnp.int32),
            pltpu.VMEM((1, BLK), jnp.int32),
            pltpu.SMEM((4, 4), jnp.int32),
            pltpu.SMEM((4,), jnp.float32),
            pltpu.SMEM((4, 4), jnp.float32),
            pltpu.SMEM((1,), jnp.int32),
            pltpu.SMEM((1,), jnp.float32),
            pltpu.VMEM((BLK, BLK), jnp.float32),
            pltpu.VMEM((BLK, BLK), jnp.float32),
            pltpu.VMEM((BLK, BLK), jnp.int16),
            pltpu.VMEM((BLK, BLK), jnp.int16),
            pltpu.VMEM((4, BLK, BLK), jnp.int16),
            pltpu.VMEM((7, BLK, BLK), jnp.int16),
            pltpu.SemaphoreType.DMA((11,)),
            pltpu.SemaphoreType.DMA((RIGHT_CHUNKS,)),
            pltpu.SemaphoreType.DMA((4, RIGHT_CHUNKS)),
            pltpu.SemaphoreType.DMA((LEFT_CHUNKS,)),
            pltpu.SemaphoreType.DMA((7, LEFT_CHUNKS)),
        ],
        compiler_params=pltpu.CompilerParams(
            collective_id=0, has_side_effects=True, vmem_limit_bytes=62 * 1024 * 1024
        ),
        name="outside_window",
    )(*args)


def solution(mesh):
    placed = (P("row", "col"),) * 3 + (P(None, "col"),) * 4 + (P(),) * 4
    return jax.shard_map(
        per_device,
        mesh=mesh,
        in_specs=placed,
        out_specs=(P("row", "col"), P("row", "col")),
        check_vma=False,
    )
```

```python
import functools
import math

import jax
import jax.numpy as jnp
from jax import lax
from jax.experimental import pallas as pl
from jax.experimental.pallas import tpu as pltpu
from jax.sharding import PartitionSpec as P

MESH = pl.DeviceIdType.MESH
BLK = 512
ROWS = 8
COLS = 32
RIGHT_CHUNK = 32
RIGHT_CHUNKS = BLK // RIGHT_CHUNK
AHEAD = 2
FIRST_ROWS = 128
LEFT_CHUNK = 64
LEFT_CHUNKS = BLK // LEFT_CHUNK
HALF_CHUNKS = LEFT_CHUNKS // 2

LOG_LOW = math.log(BLK * 0.0099**2) - 0.01
LOG_HIGH = math.log(3 * BLK * 17.5**2) + 0.01
LOG_MIDDLE = (LOG_LOW + LOG_HIGH) / 2
LOG_STEP = (LOG_HIGH - LOG_LOW) / 65534


def encode(x):
    code = jnp.round((jnp.log(x) - LOG_MIDDLE) * (1.0 / LOG_STEP))
    return jnp.clip(code, -32767.0, 32767.0).astype(jnp.int32).astype(jnp.int16)


def decode(code):
    return jnp.exp(code.astype(jnp.int32).astype(jnp.float32) * LOG_STEP + LOG_MIDDLE)


def kernel(
    outside,
    inside_head,
    inside_tail,
    inside_pair,
    seq_head_any,
    seq_tail_any,
    pair_mask_any,
    split_weight_any,
    pair_weight_any,
    span_blocks,
    partition,
    outside_out,
    prob_out,
    out_tile,
    head_tile,
    tail_tile,
    factor,
    seq_head,
    seq_tail,
    pair_mask,
    split_weight,
    pair_weight,
    right,
    left,
    right_code,
    left_code,
    right_in,
    left_in,
    load_sem,
    right_send,
    right_recv,
    share_send,
    left_send,
    left_recv,
    left_ready,
):
    row = lax.axis_index("row")
    col = lax.axis_index("col")
    core = lax.rem(row, 2)
    along = lax.rem(col - 2 * (row // 2) + 32, 8)
    reach = lax.rem(col - row + 31, 8) + 1
    is_owner = reach == 8
    owner_row = lax.rem(col, 8)
    chip_away = lax.rem(row // 2 - owner_row // 2 + 4, 4)
    at_owner_chip = chip_away == 0
    sibling = row + 1 - 2 * core

    def at_col(c):
        return (row, lax.rem(c + COLS, COLS))

    def at_row(r):
        return (lax.rem(r + ROWS, ROWS), col)

    gathers = is_owner & (core == 1)
    near = (along == 0) & (core == 1)
    has_up = (along == 2) | (along == 3) | (along == 6) | (along == 7) | gathers
    passes_on = (along >= 3) & (along <= 6)
    next_col = jnp.where(
        passes_on | near, jnp.where((along == 3) | (along == 4), col - 1, col + 1), col - reach
    )
    next_slot = jnp.where(
        passes_on | (along == 2), 0, jnp.where(along == 7, 1, jnp.where(is_owner, 3, 2))
    )
    up_slot = jnp.where(gathers, 2, 0)
    far = (along == 4) | (along == 5)
    middle = (along == 3) | (along == 6)
    last = (along == 2) | (along == 7)
    far_col = jnp.where(along == 4, col - 2, col + 2)

    loads = [
        pltpu.make_async_copy(src, dst, load_sem.at[n])
        for n, (src, dst) in enumerate(
            ((outside, out_tile), (inside_tail, tail_tile), (inside_head, head_tile))
        )
    ]
    for load in loads:
        load.start()

    barrier = pltpu.get_barrier_semaphore()

    def announce(device):
        pl.semaphore_signal(barrier, inc=1, device_id=device, device_id_type=MESH)

    @pl.when(has_up)
    def _():
        announce(at_col(jnp.where((along == 2) | (along == 3), col + 1, col - 1)))

    @pl.when(last)
    def _():
        announce(at_col(jnp.where(along == 2, col + 2, col - 2)))

    @pl.when(is_owner)
    def _():
        for away in (2 - core, 7 - core, 8):
            announce(at_col(col + away))

    @pl.when(is_owner & (core == 0))
    def _():
        announce(at_col(col + 1))

    @pl.when(jnp.logical_not(at_owner_chip & jnp.logical_not(is_owner)))
    def _():
        announce(at_row(sibling))

    @pl.when(jnp.logical_not(at_owner_chip))
    def _():
        announce(at_row(owner_row))

    loads[0].wait()
    loads[1].wait()

    def right_product(rows):
        right[rows, :] = lax.dot_general(
            out_tile[rows, :],
            tail_tile[...],
            (((1,), (1,)), ((), ())),
            preferred_element_type=jnp.float32,
        )

    right_product(slice(0, FIRST_ROWS))

    pl.semaphore_wait(barrier, jnp.where(is_owner, ROWS - 1, jnp.where(far, 3, 2)))

    @pl.when(is_owner)
    def _():
        for away in range(2, ROWS):
            pl.semaphore_signal(
                left_ready, inc=1, device_id=at_row(row - core + away), device_id_type=MESH
            )

    def right_copy(n):
        rows = pl.ds(pl.multiple_of(n * RIGHT_CHUNK, RIGHT_CHUNK), RIGHT_CHUNK)
        return pltpu.make_async_remote_copy(
            src_ref=right_code.at[rows],
            dst_ref=right_in.at[next_slot, rows],
            send_sem=right_send.at[n],
            recv_sem=right_recv.at[next_slot, n],
            device_id=at_col(next_col),
            device_id_type=MESH,
        )

    def ahead_copy(n):
        rows = pl.ds(pl.multiple_of(n * RIGHT_CHUNK, RIGHT_CHUNK), RIGHT_CHUNK)
        return pltpu.make_async_remote_copy(
            src_ref=right_code.at[rows],
            dst_ref=right_in.at[1, rows],
            send_sem=right_send.at[n],
            recv_sem=right_recv.at[1, n],
            device_id=at_col(far_col),
            device_id_type=MESH,
        )

    def right_arrival(slot, n):
        rows = pl.ds(pl.multiple_of(n * RIGHT_CHUNK, RIGHT_CHUNK), RIGHT_CHUNK)
        return pltpu.make_async_remote_copy(
            src_ref=right_code.at[rows],
            dst_ref=right_in.at[slot, rows],
            send_sem=right_send.at[n],
            recv_sem=right_recv.at[slot, n],
            device_id=at_col(next_col),
            device_id_type=MESH,
        )

    def code_rows(n):
        rows = pl.ds(pl.multiple_of(n * RIGHT_CHUNK, RIGHT_CHUNK), RIGHT_CHUNK)
        right_code[rows, :] = encode(right[rows, :])

    def send_own(n, carry):
        code_rows(n)
        right_copy(n).start()
        return carry

    def send_ahead(n, carry):
        code_rows(n)
        ahead_copy(n).start()
        return carry

    first_chunks = FIRST_ROWS // RIGHT_CHUNK

    @pl.when(far)
    def _():
        lax.fori_loop(0, AHEAD, send_ahead, 0)

    starts = jnp.logical_not(has_up)
    lax.fori_loop(
        jnp.where(far, AHEAD, 0),
        jnp.where(starts, first_chunks, jnp.where(middle, AHEAD, 0)),
        send_own,
        0,
    )
    right_product(slice(FIRST_ROWS, BLK))
    lax.fori_loop(first_chunks, jnp.where(starts, RIGHT_CHUNKS, first_chunks), send_own, 0)

    loads[2].wait()

    left[...] = lax.dot_general(
        head_tile[...],
        out_tile[...],
        (((0,), (0,)), ((), ())),
        preferred_element_type=jnp.float32,
    )

    def counts(r):
        return col >= lax.rem(col - r + 31, 8) + 1

    def left_rows(n):
        return pl.ds(pl.multiple_of(n * LEFT_CHUNK, LEFT_CHUNK), LEFT_CHUNK)

    def share_copy(n):
        return pltpu.make_async_remote_copy(
            src_ref=left_code.at[left_rows(n)],
            dst_ref=left_in.at[0, left_rows(n)],
            send_sem=share_send.at[n],
            recv_sem=left_recv.at[0, n],
            device_id=at_row(sibling),
            device_id_type=MESH,
        )

    def left_copy(n):
        return pltpu.make_async_remote_copy(
            src_ref=left_code.at[left_rows(n)],
            dst_ref=left_in.at[chip_away, left_rows(n)],
            send_sem=left_send.at[n],
            recv_sem=left_recv.at[chip_away, n],
            device_id=at_row(owner_row),
            device_id_type=MESH,
        )

    @pl.when(jnp.logical_not(is_owner))
    def _():
        def give(n, carry):
            left_code[left_rows(n), :] = encode(left[left_rows(n), :])
            share_copy(n).start()
            return carry

        first = jnp.where(at_owner_chip, 0, (1 - core) * HALF_CHUNKS)
        last = jnp.where(at_owner_chip, LEFT_CHUNKS, (2 - core) * HALF_CHUNKS)
        lax.fori_loop(first, last, give, 0)

    @pl.when(jnp.logical_not(at_owner_chip))
    def _():
        mine, theirs = counts(row), counts(sibling)
        pl.semaphore_wait(left_ready, 1)

        def merge(n, carry):
            rows = left_rows(n)
            share_copy(n).wait_recv()
            total = jnp.where(mine, left[rows, :], 0.0)
            total = total + jnp.where(theirs, decode(left_in[0, rows, :]), 0.0)
            left_code[rows, :] = encode(jnp.where(mine | theirs, total, 1.0))
            left_copy(n).start()
            return carry

        lax.fori_loop(core * HALF_CHUNKS, (core + 1) * HALF_CHUNKS, merge, 0)

    @pl.when(last)
    def _():
        def step(n, carry):
            rows = pl.ds(pl.multiple_of(n * RIGHT_CHUNK, RIGHT_CHUNK), RIGHT_CHUNK)
            right_arrival(0, n).wait_recv()
            right_arrival(1, n).wait_recv()
            total = right[rows, :] + decode(right_in[0, rows, :]) + decode(right_in[1, rows, :])
            right_code[rows, :] = encode(total)
            right_copy(n).start()
            return carry

        lax.fori_loop(0, AHEAD, step, 0)

    @pl.when(has_up)
    def _():
        def step(n, carry):
            rows = pl.ds(pl.multiple_of(n * RIGHT_CHUNK, RIGHT_CHUNK), RIGHT_CHUNK)
            right_arrival(up_slot, n).wait_recv()
            right_code[rows, :] = encode(right[rows, :] + decode(right_in[up_slot, rows, :]))
            right_copy(n).start()
            return carry

        lax.fori_loop(jnp.where(gathers, 0, AHEAD), RIGHT_CHUNKS, step, 0)

    @pl.when(jnp.logical_not(is_owner))
    def _():
        outside_out[...] = jnp.zeros((BLK, BLK), jnp.float32)
        prob_out[...] = jnp.zeros((BLK, BLK), jnp.float32)

    @pl.when(is_owner)
    def _():
        owner_loads = [
            pltpu.make_async_copy(src, dst, load_sem.at[3 + n])
            for n, (src, dst) in enumerate(
                (
                    (inside_pair, factor),
                    (seq_head_any, seq_head),
                    (seq_tail_any, seq_tail),
                    (pair_mask_any, pair_mask),
                    (split_weight_any, split_weight),
                    (pair_weight_any, pair_weight),
                )
            )
        ]
        for load in owner_loads:
            load.start()
        for load in owner_loads:
            load.wait()
        head_codes = jnp.transpose(
            jnp.broadcast_to(seq_head[...].astype(jnp.float32), (8, BLK)), (1, 0)
        )[:, :1]
        tail_codes = seq_tail[...]

        def chosen(codes, values):
            picked = jnp.where(codes == 1, values[1], values[0])
            picked = jnp.where(codes == 2, values[2], picked)
            return jnp.where(codes == 3, values[3], picked)

        weights = [split_weight[n] for n in range(4)]
        tail_weight = chosen(tail_codes, weights)
        pair_rows = [chosen(tail_codes, [pair_weight[h, t] for t in range(4)]) for h in range(4)]
        lane = lax.broadcasted_iota(jnp.int32, (1, BLK), 1)
        span_nt = BLK * span_blocks[0].astype(jnp.float32)

        blocks = [slice(n * 128, n * 128 + 128) for n in range(4)]
        for rows in blocks:
            codes = head_codes[rows]
            table = chosen(codes, pair_rows)
            place = lax.broadcasted_iota(jnp.int32, (128, BLK), 0) + rows.start
            across = lax.broadcasted_iota(jnp.int32, (128, BLK), 1)
            span = span_nt + (across - place).astype(jnp.float32)
            penalty = jnp.sqrt(64.0 * BLK / span)
            factor[rows, :] = factor[rows, :] * table * penalty / partition[0]

        def left_arrival(slot, n):
            return pltpu.make_async_remote_copy(
                src_ref=left_code.at[left_rows(n)],
                dst_ref=left_in.at[slot, left_rows(n)],
                send_sem=left_send.at[n],
                recv_sem=left_recv.at[slot, n],
                device_id=at_row(sibling),
                device_id_type=MESH,
            )

        def right_near(n, carry):
            rows = pl.ds(pl.multiple_of(n * RIGHT_CHUNK, RIGHT_CHUNK), RIGHT_CHUNK)
            right_arrival(3, n).wait_recv()
            right[rows, :] = decode(right_in[3, rows, :])
            return carry

        def right_side(n, carry):
            rows = pl.ds(pl.multiple_of(n * RIGHT_CHUNK, RIGHT_CHUNK), RIGHT_CHUNK)
            right_arrival(2, n).wait_recv()
            right[rows, :] += decode(right_in[2, rows, :])
            return carry

        def left_add(n, carry):
            rows = left_rows(n)
            total = jnp.where(counts(row), left[rows, :], 0.0)
            for slot in range(4):
                there = lax.rem(row - core + 2 * slot, ROWS)
                some = counts(sibling) if slot == 0 else counts(there) | counts(there + 1)
                left_arrival(slot, n).wait_recv()
                total = total + jnp.where(some, decode(left_in[slot, rows, :]), 0.0)
            left[rows, :] = total
            return carry

        lax.fori_loop(0, RIGHT_CHUNKS, right_near, 0)

        @pl.when(core == 0)
        def _():
            lax.fori_loop(0, RIGHT_CHUNKS, right_side, 0)

        lax.fori_loop(0, LEFT_CHUNKS, left_add, 0)

        for b, rows in enumerate(blocks):
            codes = head_codes[rows]
            head_weight = chosen(codes, weights)
            allowed = chosen(lane // 128, [pair_mask[b, n].astype(jnp.float32) for n in range(4)])
            for part in range(128 // RIGHT_CHUNK):
                n = b * (128 // RIGHT_CHUNK) + part
                here = slice(n * RIGHT_CHUNK, (n + 1) * RIGHT_CHUNK)
                inner = slice(part * RIGHT_CHUNK, (part + 1) * RIGHT_CHUNK)
                right_arrival(0, n).wait_recv()
                right_arrival(1, n).wait_recv()
                right_sum = right[here, :] + decode(right_in[0, here, :]) + decode(right_in[1, here, :])
                diag = (
                    allowed
                    * (right_sum * tail_weight + head_weight[inner] * left[here, :])
                    * (1.0 / BLK)
                )
                outside_out[here, :] = diag
                prob_out[here, :] = diag * factor[here, :]

    def sent(n, carry):
        right_copy(n).wait_send()
        return carry

    lax.fori_loop(0, RIGHT_CHUNKS, sent, 0)

    @pl.when(jnp.logical_not(is_owner))
    def _():
        def given(n, carry):
            share_copy(n).wait_send()
            return carry

        first = jnp.where(at_owner_chip, 0, (1 - core) * HALF_CHUNKS)
        last = jnp.where(at_owner_chip, LEFT_CHUNKS, (2 - core) * HALF_CHUNKS)
        lax.fori_loop(first, last, given, 0)

    @pl.when(jnp.logical_not(at_owner_chip))
    def _():
        def handed_over(n, carry):
            left_copy(n).wait_send()
            return carry

        lax.fori_loop(core * HALF_CHUNKS, (core + 1) * HALF_CHUNKS, handed_over, 0)


def put_out(diag, prob, outside_out, prob_out, sem):
    copies = [
        pltpu.make_async_copy(src, dst, sem.at[n])
        for n, (src, dst) in enumerate(((diag, outside_out), (prob, prob_out)))
    ]
    for copy in copies:
        copy.start()
    for copy in copies:
        copy.wait()


def per_device(*args):
    vmem = pl.BlockSpec(memory_space=pltpu.VMEM)
    smem = pl.BlockSpec(memory_space=pltpu.SMEM)
    hbm = pl.BlockSpec(memory_space=pltpu.HBM)
    tile = pltpu.VMEM((BLK, BLK), jnp.float32)
    results = pl.pallas_call(
        kernel,
        out_shape=(tile, tile),
        in_specs=[hbm] * 9 + [smem] * 2,
        out_specs=(vmem, vmem),
        scratch_shapes=[
            pltpu.VMEM((BLK, BLK), jnp.bfloat16),
            pltpu.VMEM((BLK, BLK), jnp.bfloat16),
            pltpu.VMEM((BLK, BLK), jnp.bfloat16),
            pltpu.VMEM((BLK, BLK), jnp.float32),
            pltpu.VMEM((1, BLK), jnp.int32),
            pltpu.VMEM((1, BLK), jnp.int32),
            pltpu.SMEM((4, 4), jnp.int32),
            pltpu.SMEM((4,), jnp.float32),
            pltpu.SMEM((4, 4), jnp.float32),
            pltpu.VMEM((BLK, BLK), jnp.float32),
            pltpu.VMEM((BLK, BLK), jnp.float32),
            pltpu.VMEM((BLK, BLK), jnp.int16),
            pltpu.VMEM((BLK, BLK), jnp.int16),
            pltpu.VMEM((4, BLK, BLK), jnp.int16),
            pltpu.VMEM((4, BLK, BLK), jnp.int16),
            pltpu.SemaphoreType.DMA((11,)),
            pltpu.SemaphoreType.DMA((RIGHT_CHUNKS,)),
            pltpu.SemaphoreType.DMA((4, RIGHT_CHUNKS)),
            pltpu.SemaphoreType.DMA((LEFT_CHUNKS,)),
            pltpu.SemaphoreType.DMA((LEFT_CHUNKS,)),
            pltpu.SemaphoreType.DMA((4, LEFT_CHUNKS)),
            pltpu.SemaphoreType.REGULAR,
        ],
        compiler_params=pltpu.CompilerParams(
            collective_id=0, has_side_effects=True, vmem_limit_bytes=62400 * 1024
        ),
        name="outside_window",
    )(*args)
    tile = jax.ShapeDtypeStruct((BLK, BLK), jnp.float32)
    return pl.pallas_call(
        put_out,
        out_shape=(tile, tile),
        in_specs=[vmem] * 2,
        out_specs=(hbm, hbm),
        scratch_shapes=[pltpu.SemaphoreType.DMA((2,))],
        compiler_params=pltpu.CompilerParams(vmem_limit_bytes=1024 * 1024),
        name="put_out",
    )(*results)


def solution(mesh):
    placed = (P("row", "col"),) * 3 + (P(None, "col"),) * 4 + (P(),) * 4
    return jax.shard_map(
        per_device,
        mesh=mesh,
        in_specs=placed,
        out_specs=(P("row", "col"), P("row", "col")),
        check_vma=False,
    )
```

```python
import functools
import math

import jax
import jax.numpy as jnp
from jax import lax
from jax.experimental import pallas as pl
from jax.experimental.pallas import tpu as pltpu
from jax.sharding import PartitionSpec as P

MESH = pl.DeviceIdType.MESH
BLK = 512
ROWS = 8
COLS = 32
RIGHT_CHUNK = 32
RIGHT_CHUNKS = BLK // RIGHT_CHUNK
SHORT = 5
LEFT_CHUNK = 64
LEFT_CHUNKS = BLK // LEFT_CHUNK
HALF_CHUNKS = LEFT_CHUNKS // 2

LOG_LOW = math.log(BLK * 0.0099**2) - 0.01
LOG_HIGH = math.log(5 * BLK * 17.5**2) + 0.01
LOG_MIDDLE = (LOG_LOW + LOG_HIGH) / 2
LOG_STEP = (LOG_HIGH - LOG_LOW) / 65534


def encode(x):
    code = jnp.round((jnp.log(x) - LOG_MIDDLE) * (1.0 / LOG_STEP))
    return jnp.clip(code, -32767.0, 32767.0).astype(jnp.int32).astype(jnp.int16)


def decode(code):
    return jnp.exp(code.astype(jnp.int32).astype(jnp.float32) * LOG_STEP + LOG_MIDDLE)


def kernel(
    outside,
    inside_head,
    inside_tail,
    inside_pair,
    seq_head_any,
    seq_tail_any,
    pair_mask_any,
    split_weight_any,
    pair_weight_any,
    span_blocks,
    partition,
    outside_out,
    prob_out,
    out_tile,
    head_tile,
    tail_tile,
    factor,
    right_weight,
    left_weight,
    seq_head,
    seq_tail,
    pair_mask,
    split_weight,
    pair_weight,
    right,
    left,
    right_code,
    left_code,
    right_in,
    left_in,
    load_sem,
    right_send,
    right_recv,
    share_send,
    left_send,
    left_recv,
    left_ready,
):
    row = lax.axis_index("row")
    col = lax.axis_index("col")
    core = lax.rem(row, 2)
    along = lax.rem(col - 2 * (row // 2) + 32, 8)
    reach = lax.rem(col - row + 31, 8) + 1
    is_owner = reach == 8
    owner_row = lax.rem(col, 8)
    chip_away = lax.rem(row // 2 - owner_row // 2 + 4, 4)
    at_owner_chip = chip_away == 0
    sibling = row + 1 - 2 * core
    early = owner_row < 4

    def at_col(c):
        return (row, lax.rem(c + COLS, COLS))

    def at_row(r):
        return (lax.rem(r + ROWS, ROWS), col)

    upward = (along >= 5) | (along == 0)
    depth = jnp.where(upward, 9 - along, along)
    toward = jnp.where(upward, col + 1, col - 1)
    behind = jnp.where(upward, col - 1, col + 1)
    first_tile, second_tile, third_tile = depth == 2, depth == 3, depth == 4
    beside = along <= 1
    beside_col = jnp.where(along == 0, col - 1, jnp.where(core == 0, col + 1, col - 7))
    next_col = jnp.where(beside, beside_col, jnp.where(first_tile, col - reach, toward))
    next_slot = jnp.where(beside | (first_tile & upward), 1, 0)

    loads = [
        pltpu.make_async_copy(src, dst, load_sem.at[n])
        for n, (src, dst) in enumerate(
            ((outside, out_tile), (inside_tail, tail_tile), (inside_head, head_tile))
        )
    ]
    for load in loads:
        load.start()

    barrier = pltpu.get_barrier_semaphore()

    def announce(device):
        pl.semaphore_signal(barrier, inc=1, device_id=device, device_id_type=MESH)

    @pl.when(first_tile | second_tile | third_tile)
    def _():
        announce(at_col(behind))

    @pl.when(first_tile)
    def _():
        announce(at_col(jnp.where(along == 7, col + 1, jnp.where(core == 0, col - 1, col + 7))))

    @pl.when(is_owner)
    def _():
        for away in (2 - core, 7 - core):
            announce(at_col(col + away))

    @pl.when(jnp.logical_not(at_owner_chip & jnp.logical_not(is_owner)))
    def _():
        announce(at_row(sibling))

    @pl.when(jnp.logical_not(at_owner_chip | early))
    def _():
        announce(at_row(owner_row))

    @pl.when(is_owner & early)
    def _():
        for away in range(2, ROWS):
            announce(at_row(row - core + away))

    loads[0].wait()
    loads[1].wait()

    right[...] = lax.dot_general(
        out_tile[...],
        tail_tile[...],
        (((1,), (1,)), ((), ())),
        preferred_element_type=jnp.float32,
    )

    others = jnp.where(third_tile, 3, 2) + jnp.where(early & jnp.logical_not(at_owner_chip), 1, 0)
    pl.semaphore_wait(barrier, jnp.where(is_owner, jnp.where(early, 1, ROWS - 1), others))

    @pl.when(is_owner & jnp.logical_not(early))
    def _():
        for away in range(2, ROWS):
            pl.semaphore_signal(
                left_ready, inc=1, device_id=at_row(row - core + away), device_id_type=MESH
            )

    def right_rows(n):
        return pl.ds(pl.multiple_of(n * RIGHT_CHUNK, RIGHT_CHUNK), RIGHT_CHUNK)

    def right_copy(n):
        return pltpu.make_async_remote_copy(
            src_ref=right_code.at[right_rows(n)],
            dst_ref=right_in.at[next_slot, right_rows(n)],
            send_sem=right_send.at[n],
            recv_sem=right_recv.at[next_slot, n],
            device_id=at_col(next_col),
            device_id_type=MESH,
        )

    def across_copy(n):
        return pltpu.make_async_remote_copy(
            src_ref=right_code.at[right_rows(n)],
            dst_ref=right_in.at[0, right_rows(n)],
            send_sem=right_send.at[n],
            recv_sem=right_recv.at[0, n],
            device_id=at_col(behind),
            device_id_type=MESH,
        )

    def right_arrival(slot, n):
        return pltpu.make_async_remote_copy(
            src_ref=right_code.at[right_rows(n)],
            dst_ref=right_in.at[slot, right_rows(n)],
            send_sem=right_send.at[n],
            recv_sem=right_recv.at[slot, n],
            device_id=at_col(next_col),
            device_id_type=MESH,
        )

    def chunk(m):
        return jnp.where(upward, RIGHT_CHUNKS - 1 - m, m)

    def send_across(m, carry):
        n = chunk(SHORT - 1 - m)
        right_code[right_rows(n), :] = encode(right[right_rows(n), :])
        across_copy(n).start()
        return carry

    def send_own(m, carry):
        n = chunk(m)
        right_code[right_rows(n), :] = encode(right[right_rows(n), :])
        right_copy(n).start()
        return carry

    @pl.when(third_tile)
    def _():
        lax.fori_loop(0, SHORT, send_across, 0)

    own_from = jnp.where(third_tile, SHORT, 0)
    own_to = jnp.where(
        first_tile,
        0,
        jnp.where(
            second_tile, SHORT, jnp.where(third_tile, RIGHT_CHUNKS - SHORT, RIGHT_CHUNKS)
        ),
    )
    lax.fori_loop(own_from, own_to, send_own, 0)

    loads[2].wait()

    left[...] = lax.dot_general(
        head_tile[...],
        out_tile[...],
        (((0,), (0,)), ((), ())),
        preferred_element_type=jnp.float32,
    )

    def counts(r):
        return col >= lax.rem(col - r + 31, 8) + 1

    def left_rows(n):
        return pl.ds(pl.multiple_of(n * LEFT_CHUNK, LEFT_CHUNK), LEFT_CHUNK)

    def share_copy(n):
        return pltpu.make_async_remote_copy(
            src_ref=left_code.at[left_rows(n)],
            dst_ref=left_in.at[0, left_rows(n)],
            send_sem=share_send.at[n],
            recv_sem=left_recv.at[0, n],
            device_id=at_row(sibling),
            device_id_type=MESH,
        )

    def left_copy(n):
        return pltpu.make_async_remote_copy(
            src_ref=left_code.at[left_rows(n)],
            dst_ref=left_in.at[chip_away, left_rows(n)],
            send_sem=left_send.at[n],
            recv_sem=left_recv.at[chip_away, n],
            device_id=at_row(owner_row),
            device_id_type=MESH,
        )

    @pl.when(jnp.logical_not(is_owner))
    def _():
        def give(n, carry):
            left_code[left_rows(n), :] = encode(left[left_rows(n), :])
            share_copy(n).start()
            return carry

        first = jnp.where(at_owner_chip, 0, (1 - core) * HALF_CHUNKS)
        last = jnp.where(at_owner_chip, LEFT_CHUNKS, (2 - core) * HALF_CHUNKS)
        lax.fori_loop(first, last, give, 0)

    @pl.when(jnp.logical_not(at_owner_chip))
    def _():
        mine, theirs = counts(row), counts(sibling)

        @pl.when(jnp.logical_not(early))
        def _():
            pl.semaphore_wait(left_ready, 1)


        def merge(n, carry):
            rows = left_rows(n)
            share_copy(n).wait_recv()
            total = jnp.where(mine, left[rows, :], 0.0)
            total = total + jnp.where(theirs, decode(left_in[0, rows, :]), 0.0)
            left_code[rows, :] = encode(jnp.where(mine | theirs, total, 1.0))
            left_copy(n).start()
            return carry

        lax.fori_loop(core * HALF_CHUNKS, (core + 1) * HALF_CHUNKS, merge, 0)

    def pass_on(m, carry):
        n = chunk(m)
        rows = right_rows(n)
        right_arrival(0, n).wait_recv()
        right_code[rows, :] = encode(right[rows, :] + decode(right_in[0, rows, :]))
        right_copy(n).start()
        return carry

    def pass_on_both(m, carry):
        n = chunk(m)
        rows = right_rows(n)
        right_arrival(1, n).wait_recv()
        total = right[rows, :] + decode(right_in[1, rows, :])
        right_arrival(0, n).wait_recv()
        right_code[rows, :] = encode(total + decode(right_in[0, rows, :]))
        right_copy(n).start()
        return carry

    @pl.when(first_tile)
    def _():
        lax.fori_loop(0, RIGHT_CHUNKS, pass_on_both, 0)

    @pl.when(second_tile | third_tile)
    def _():
        lax.fori_loop(own_to, RIGHT_CHUNKS, pass_on, 0)

    @pl.when(jnp.logical_not(is_owner))
    def _():
        outside_out[...] = jnp.zeros((BLK, BLK), jnp.float32)
        prob_out[...] = jnp.zeros((BLK, BLK), jnp.float32)

    @pl.when(is_owner)
    def _():
        owner_loads = [
            pltpu.make_async_copy(src, dst, load_sem.at[3 + n])
            for n, (src, dst) in enumerate(
                (
                    (inside_pair, factor),
                    (seq_head_any, seq_head),
                    (seq_tail_any, seq_tail),
                    (pair_mask_any, pair_mask),
                    (split_weight_any, split_weight),
                    (pair_weight_any, pair_weight),
                )
            )
        ]
        for load in owner_loads:
            load.start()
        for load in owner_loads:
            load.wait()
        head_codes = jnp.transpose(
            jnp.broadcast_to(seq_head[...].astype(jnp.float32), (8, BLK)), (1, 0)
        )[:, :1]
        tail_codes = seq_tail[...]

        def chosen(codes, values):
            picked = jnp.where(codes == 1, values[1], values[0])
            picked = jnp.where(codes == 2, values[2], picked)
            return jnp.where(codes == 3, values[3], picked)

        weights = [split_weight[n] for n in range(4)]
        tail_weight = chosen(tail_codes, weights)
        pair_rows = [chosen(tail_codes, [pair_weight[h, t] for t in range(4)]) for h in range(4)]
        lane = lax.broadcasted_iota(jnp.int32, (1, BLK), 1)
        span_nt = BLK * span_blocks[0].astype(jnp.float32)

        for b in range(4):
            rows = slice(b * 128, b * 128 + 128)
            codes = head_codes[rows]
            table = chosen(codes, pair_rows)
            place = lax.broadcasted_iota(jnp.int32, (128, BLK), 0) + rows.start
            across = lax.broadcasted_iota(jnp.int32, (128, BLK), 1)
            span = span_nt + (across - place).astype(jnp.float32)
            penalty = jnp.sqrt(64.0 * BLK / span)
            factor[rows, :] = factor[rows, :] * table * penalty / partition[0]
            allowed = chosen(lane // 128, [pair_mask[b, n].astype(jnp.float32) for n in range(4)])
            allowed = allowed * (1.0 / BLK)
            right_weight[rows, :] = jnp.broadcast_to(allowed * tail_weight, (128, BLK))
            left_weight[rows, :] = allowed * chosen(codes, weights)

        def left_arrival(slot, n):
            return pltpu.make_async_remote_copy(
                src_ref=left_code.at[left_rows(n)],
                dst_ref=left_in.at[slot, left_rows(n)],
                send_sem=left_send.at[n],
                recv_sem=left_recv.at[slot, n],
                device_id=at_row(sibling),
                device_id_type=MESH,
            )

        def arrive(slot, n):
            right_arrival(slot, n).wait_recv()
            return decode(right_in[slot, right_rows(n), :])

        def half_way(m, carry):
            for slot, n in ((0, m), (1, RIGHT_CHUNKS - 1 - m)):
                right[right_rows(n), :] = arrive(slot, n)
            return carry

        def finish(m, carry):
            for slot, n in ((0, m), (1, RIGHT_CHUNKS - 1 - m)):
                rows = right_rows(n)
                right_sum = right[rows, :] + arrive(slot, n)
                diag = right_sum * right_weight[rows, :] + left[rows, :]
                outside_out[rows, :] = diag
                prob_out[rows, :] = diag * factor[rows, :]
            return carry

        def left_add(n, carry):
            rows = left_rows(n)
            total = jnp.where(counts(row), left[rows, :], 0.0)
            for slot in range(4):
                there = lax.rem(row - core + 2 * slot, ROWS)
                some = counts(sibling) if slot == 0 else counts(there) | counts(there + 1)
                left_arrival(slot, n).wait_recv()
                total = total + jnp.where(some, decode(left_in[slot, rows, :]), 0.0)
            left[rows, :] = total * left_weight[rows, :]
            return carry

        lax.fori_loop(0, LEFT_CHUNKS, left_add, 0)

        lax.fori_loop(0, RIGHT_CHUNKS // 2, half_way, 0)
        lax.fori_loop(RIGHT_CHUNKS // 2, RIGHT_CHUNKS, finish, 0)

    def sent(n, carry):
        right_copy(n).wait_send()
        return carry

    lax.fori_loop(0, RIGHT_CHUNKS, sent, 0)

    @pl.when(jnp.logical_not(is_owner))
    def _():
        def given(n, carry):
            share_copy(n).wait_send()
            return carry

        first = jnp.where(at_owner_chip, 0, (1 - core) * HALF_CHUNKS)
        last = jnp.where(at_owner_chip, LEFT_CHUNKS, (2 - core) * HALF_CHUNKS)
        lax.fori_loop(first, last, given, 0)

    @pl.when(jnp.logical_not(at_owner_chip))
    def _():
        def handed_over(n, carry):
            left_copy(n).wait_send()
            return carry

        lax.fori_loop(core * HALF_CHUNKS, (core + 1) * HALF_CHUNKS, handed_over, 0)


def put_out(diag, prob, outside_out, prob_out, sem):
    copies = [
        pltpu.make_async_copy(src, dst, sem.at[n])
        for n, (src, dst) in enumerate(((diag, outside_out), (prob, prob_out)))
    ]
    for copy in copies:
        copy.start()
    for copy in copies:
        copy.wait()


def per_device(*args):
    vmem = pl.BlockSpec(memory_space=pltpu.VMEM)
    smem = pl.BlockSpec(memory_space=pltpu.SMEM)
    hbm = pl.BlockSpec(memory_space=pltpu.HBM)
    tile = pltpu.VMEM((BLK, BLK), jnp.float32)
    results = pl.pallas_call(
        kernel,
        out_shape=(tile, tile),
        in_specs=[hbm] * 9 + [smem] * 2,
        out_specs=(vmem, vmem),
        scratch_shapes=[
            pltpu.VMEM((BLK, BLK), jnp.bfloat16),
            pltpu.VMEM((BLK, BLK), jnp.bfloat16),
            pltpu.VMEM((BLK, BLK), jnp.bfloat16),
            pltpu.VMEM((BLK, BLK), jnp.float32),
            pltpu.VMEM((BLK, BLK), jnp.float32),
            pltpu.VMEM((BLK, BLK), jnp.float32),
            pltpu.VMEM((1, BLK), jnp.int32),
            pltpu.VMEM((1, BLK), jnp.int32),
            pltpu.SMEM((4, 4), jnp.int32),
            pltpu.SMEM((4,), jnp.float32),
            pltpu.SMEM((4, 4), jnp.float32),
            pltpu.VMEM((BLK, BLK), jnp.float32),
            pltpu.VMEM((BLK, BLK), jnp.float32),
            pltpu.VMEM((BLK, BLK), jnp.int16),
            pltpu.VMEM((BLK, BLK), jnp.int16),
            pltpu.VMEM((2, BLK, BLK), jnp.int16),
            pltpu.VMEM((4, BLK, BLK), jnp.int16),
            pltpu.SemaphoreType.DMA((11,)),
            pltpu.SemaphoreType.DMA((RIGHT_CHUNKS,)),
            pltpu.SemaphoreType.DMA((2, RIGHT_CHUNKS)),
            pltpu.SemaphoreType.DMA((LEFT_CHUNKS,)),
            pltpu.SemaphoreType.DMA((LEFT_CHUNKS,)),
            pltpu.SemaphoreType.DMA((4, LEFT_CHUNKS)),
            pltpu.SemaphoreType.REGULAR,
        ],
        compiler_params=pltpu.CompilerParams(
            collective_id=0, has_side_effects=True, vmem_limit_bytes=62400 * 1024
        ),
        name="outside_window",
    )(*args)
    tile = jax.ShapeDtypeStruct((BLK, BLK), jnp.float32)
    return pl.pallas_call(
        put_out,
        out_shape=(tile, tile),
        in_specs=[vmem] * 2,
        out_specs=(hbm, hbm),
        scratch_shapes=[pltpu.SemaphoreType.DMA((2,))],
        compiler_params=pltpu.CompilerParams(vmem_limit_bytes=1024 * 1024),
        name="put_out",
    )(*results)


def solution(mesh):
    placed = (P("row", "col"),) * 3 + (P(None, "col"),) * 4 + (P(),) * 4
    return jax.shard_map(
        per_device,
        mesh=mesh,
        in_specs=placed,
        out_specs=(P("row", "col"), P("row", "col")),
        check_vma=False,
    )
```

```python
import functools
import math

import jax
import jax.numpy as jnp
from jax import lax
from jax.experimental import pallas as pl
from jax.experimental.pallas import tpu as pltpu
from jax.sharding import PartitionSpec as P

MESH = pl.DeviceIdType.MESH
BLK = 512
ROWS = 8
COLS = 32
RIGHT_CHUNK = 32
RIGHT_CHUNKS = BLK // RIGHT_CHUNK
SHORT = 5
LEFT_CHUNK = 64
LEFT_CHUNKS = BLK // LEFT_CHUNK
HALF_CHUNKS = LEFT_CHUNKS // 2

LOG_LOW = math.log(BLK * 0.0099**2) - 0.01
LOG_HIGH = math.log(5 * BLK * 17.5**2) + 0.01
LOG_MIDDLE = (LOG_LOW + LOG_HIGH) / 2
LOG_STEP = (LOG_HIGH - LOG_LOW) / 65534


def encode(x):
    code = jnp.round((jnp.log(x) - LOG_MIDDLE) * (1.0 / LOG_STEP))
    return jnp.clip(code, -32767.0, 32767.0).astype(jnp.int32).astype(jnp.int16)


def decode(code):
    return jnp.exp(code.astype(jnp.int32).astype(jnp.float32) * LOG_STEP + LOG_MIDDLE)


def kernel(
    outside,
    inside_head,
    inside_tail,
    inside_pair,
    seq_head_any,
    seq_tail_any,
    pair_mask_any,
    split_weight_any,
    pair_weight_any,
    span_blocks,
    partition,
    outside_out,
    prob_out,
    out_tile,
    head_tile,
    tail_tile,
    factor,
    right_weight,
    left_weight,
    seq_head,
    seq_tail,
    pair_mask,
    split_weight,
    pair_weight,
    right,
    left,
    right_code,
    left_code,
    right_in,
    left_in,
    load_sem,
    right_send,
    right_recv,
    share_send,
    left_send,
    left_recv,
    left_ready,
    chain_ready,
):
    row = lax.axis_index("row")
    col = lax.axis_index("col")
    core = lax.rem(row, 2)
    along = lax.rem(col - 2 * (row // 2) + 32, 8)
    reach = lax.rem(col - row + 31, 8) + 1
    is_owner = reach == 8
    owner_row = lax.rem(col, 8)
    chip_away = lax.rem(row // 2 - owner_row // 2 + 4, 4)
    at_owner_chip = chip_away == 0
    sibling = row + 1 - 2 * core
    early = owner_row < 4
    chip_row = row // 2
    waits = (owner_row == 0) & (chip_row >= 2)
    tells = ((chip_row == 2) & (along == 3)) | ((chip_row == 3) & is_owner)
    told_col = jnp.where(is_owner, col + 2 - core, col + 1)

    def at_col(c):
        return (row, lax.rem(c + COLS, COLS))

    def at_row(r):
        return (lax.rem(r + ROWS, ROWS), col)

    upward = (along >= 5) | (along == 0)
    depth = jnp.where(upward, 9 - along, along)
    toward = jnp.where(upward, col + 1, col - 1)
    behind = jnp.where(upward, col - 1, col + 1)
    first_tile, second_tile, third_tile = depth == 2, depth == 3, depth == 4
    beside = along <= 1
    beside_col = jnp.where(along == 0, col - 1, jnp.where(core == 0, col + 1, col - 7))
    wraps = row < 2
    straight = wraps & (along == 0)
    joined = first_tile & jnp.logical_not(wraps & (along == 7))
    beside_col = jnp.where(straight, col - reach, beside_col)
    next_col = jnp.where(beside, beside_col, jnp.where(first_tile, col - reach, toward))
    next_slot = jnp.where(straight, 2, jnp.where(beside | (first_tile & upward), 1, 0))

    loads = [
        pltpu.make_async_copy(src, dst, load_sem.at[n])
        for n, (src, dst) in enumerate(
            ((outside, out_tile), (inside_tail, tail_tile), (inside_head, head_tile))
        )
    ]
    for load in loads:
        load.start()

    barrier = pltpu.get_barrier_semaphore()

    def announce(device):
        pl.semaphore_signal(barrier, inc=1, device_id=device, device_id_type=MESH)

    @pl.when((first_tile | second_tile | third_tile) & jnp.logical_not(tells))
    def _():
        announce(at_col(behind))

    @pl.when(waits)
    def _():
        announce(at_col(next_col))

    @pl.when(is_owner & wraps)
    def _():
        announce(at_col(col + 8 - core))

    @pl.when(joined)
    def _():
        announce(at_col(jnp.where(along == 7, col + 1, jnp.where(core == 0, col - 1, col + 7))))

    @pl.when(is_owner)
    def _():
        announce(at_col(col + 7 - core))

    @pl.when(is_owner & jnp.logical_not(tells))
    def _():
        announce(at_col(col + 2 - core))

    @pl.when(jnp.logical_not(at_owner_chip & jnp.logical_not(is_owner)))
    def _():
        announce(at_row(sibling))

    @pl.when(jnp.logical_not(at_owner_chip | early))
    def _():
        announce(at_row(owner_row))

    @pl.when(is_owner & early)
    def _():
        for away in range(2, ROWS):
            announce(at_row(row - core + away))

    loads[0].wait()
    loads[1].wait()

    right[...] = lax.dot_general(
        out_tile[...],
        tail_tile[...],
        (((1,), (1,)), ((), ())),
        preferred_element_type=jnp.float32,
    )

    others = jnp.where(third_tile, 3, 2) + jnp.where(early & jnp.logical_not(at_owner_chip), 1, 0)
    arrivals = jnp.where(is_owner, jnp.where(early, 1, ROWS - 1), others)
    pl.semaphore_wait(barrier, arrivals + jnp.where(tells, 1, 0) - jnp.where(waits, 1, 0))

    @pl.when(tells)
    def _():
        pl.semaphore_signal(chain_ready, inc=1, device_id=at_col(told_col), device_id_type=MESH)

    @pl.when(is_owner & jnp.logical_not(early))
    def _():
        for away in range(2, ROWS):
            pl.semaphore_signal(
                left_ready, inc=1, device_id=at_row(row - core + away), device_id_type=MESH
            )

    def right_rows(n):
        return pl.ds(pl.multiple_of(n * RIGHT_CHUNK, RIGHT_CHUNK), RIGHT_CHUNK)

    def right_copy(n):
        return pltpu.make_async_remote_copy(
            src_ref=right_code.at[right_rows(n)],
            dst_ref=right_in.at[next_slot, right_rows(n)],
            send_sem=right_send.at[n],
            recv_sem=right_recv.at[next_slot, n],
            device_id=at_col(next_col),
            device_id_type=MESH,
        )

    def across_copy(n):
        return pltpu.make_async_remote_copy(
            src_ref=right_code.at[right_rows(n)],
            dst_ref=right_in.at[0, right_rows(n)],
            send_sem=right_send.at[n],
            recv_sem=right_recv.at[0, n],
            device_id=at_col(behind),
            device_id_type=MESH,
        )

    def right_arrival(slot, n):
        return pltpu.make_async_remote_copy(
            src_ref=right_code.at[right_rows(n)],
            dst_ref=right_in.at[slot, right_rows(n)],
            send_sem=right_send.at[n],
            recv_sem=right_recv.at[slot, n],
            device_id=at_col(next_col),
            device_id_type=MESH,
        )

    def chunk(m):
        return jnp.where(upward, RIGHT_CHUNKS - 1 - m, m)

    def send_across(m, carry):
        n = chunk(SHORT - 1 - m)
        right_code[right_rows(n), :] = encode(right[right_rows(n), :])
        across_copy(n).start()
        return carry

    def send_own(m, carry):
        n = chunk(m)
        right_code[right_rows(n), :] = encode(right[right_rows(n), :])
        right_copy(n).start()
        return carry

    def counts(r):
        return col >= lax.rem(col - r + 31, 8) + 1

    def left_rows(n):
        return pl.ds(pl.multiple_of(n * LEFT_CHUNK, LEFT_CHUNK), LEFT_CHUNK)

    def share_copy(n):
        return pltpu.make_async_remote_copy(
            src_ref=left_code.at[left_rows(n)],
            dst_ref=left_in.at[0, left_rows(n)],
            send_sem=share_send.at[n],
            recv_sem=left_recv.at[0, n],
            device_id=at_row(sibling),
            device_id_type=MESH,
        )

    def left_copy(n):
        return pltpu.make_async_remote_copy(
            src_ref=left_code.at[left_rows(n)],
            dst_ref=left_in.at[chip_away, left_rows(n)],
            send_sem=left_send.at[n],
            recv_sem=left_recv.at[chip_away, n],
            device_id=at_row(owner_row),
            device_id_type=MESH,
        )

    def left_part():
        loads[2].wait()

        left[...] = lax.dot_general(
            head_tile[...],
            out_tile[...],
            (((0,), (0,)), ((), ())),
            preferred_element_type=jnp.float32,
        )

        @pl.when(jnp.logical_not(is_owner))
        def _():
            def give(n, carry):
                left_code[left_rows(n), :] = encode(left[left_rows(n), :])
                share_copy(n).start()
                return carry

            first = jnp.where(at_owner_chip, 0, (1 - core) * HALF_CHUNKS)
            last = jnp.where(at_owner_chip, LEFT_CHUNKS, (2 - core) * HALF_CHUNKS)
            lax.fori_loop(first, last, give, 0)

        @pl.when(jnp.logical_not(at_owner_chip))
        def _():
            mine, theirs = counts(row), counts(sibling)

            @pl.when(jnp.logical_not(early))
            def _():
                pl.semaphore_wait(left_ready, 1)


            def merge(n, carry):
                rows = left_rows(n)
                share_copy(n).wait_recv()
                total = jnp.where(mine, left[rows, :], 0.0)
                total = total + jnp.where(theirs, decode(left_in[0, rows, :]), 0.0)
                left_code[rows, :] = encode(jnp.where(mine | theirs, total, 1.0))
                left_copy(n).start()
                return carry

            lax.fori_loop(core * HALF_CHUNKS, (core + 1) * HALF_CHUNKS, merge, 0)

    @pl.when(waits)
    def _():
        left_part()
        pl.semaphore_wait(chain_ready, 1)

    @pl.when(third_tile)
    def _():
        lax.fori_loop(0, SHORT, send_across, 0)

    own_from = jnp.where(third_tile, SHORT, 0)
    own_to = jnp.where(
        first_tile,
        0,
        jnp.where(
            second_tile, SHORT, jnp.where(third_tile, RIGHT_CHUNKS - SHORT, RIGHT_CHUNKS)
        ),
    )
    lax.fori_loop(own_from, own_to, send_own, 0)

    @pl.when(jnp.logical_not(waits))
    def _():
        left_part()

    def pass_on(m, carry):
        n = chunk(m)
        rows = right_rows(n)
        right_arrival(0, n).wait_recv()
        right_code[rows, :] = encode(right[rows, :] + decode(right_in[0, rows, :]))
        right_copy(n).start()
        return carry

    def pass_on_both(m, carry):
        n = chunk(m)
        rows = right_rows(n)
        right_arrival(1, n).wait_recv()
        total = right[rows, :] + decode(right_in[1, rows, :])
        right_arrival(0, n).wait_recv()
        right_code[rows, :] = encode(total + decode(right_in[0, rows, :]))
        right_copy(n).start()
        return carry

    @pl.when(joined)
    def _():
        lax.fori_loop(0, RIGHT_CHUNKS, pass_on_both, 0)

    @pl.when(jnp.logical_not(joined | beside))
    def _():
        lax.fori_loop(own_to, RIGHT_CHUNKS, pass_on, 0)

    @pl.when(jnp.logical_not(is_owner))
    def _():
        outside_out[...] = jnp.zeros((BLK, BLK), jnp.float32)
        prob_out[...] = jnp.zeros((BLK, BLK), jnp.float32)

    @pl.when(is_owner)
    def _():
        owner_loads = [
            pltpu.make_async_copy(src, dst, load_sem.at[3 + n])
            for n, (src, dst) in enumerate(
                (
                    (inside_pair, factor),
                    (seq_head_any, seq_head),
                    (seq_tail_any, seq_tail),
                    (pair_mask_any, pair_mask),
                    (split_weight_any, split_weight),
                    (pair_weight_any, pair_weight),
                )
            )
        ]
        for load in owner_loads:
            load.start()
        for load in owner_loads:
            load.wait()
        head_codes = jnp.transpose(
            jnp.broadcast_to(seq_head[...].astype(jnp.float32), (8, BLK)), (1, 0)
        )[:, :1]
        tail_codes = seq_tail[...]

        def chosen(codes, values):
            picked = jnp.where(codes == 1, values[1], values[0])
            picked = jnp.where(codes == 2, values[2], picked)
            return jnp.where(codes == 3, values[3], picked)

        weights = [split_weight[n] for n in range(4)]
        tail_weight = chosen(tail_codes, weights)
        pair_rows = [chosen(tail_codes, [pair_weight[h, t] for t in range(4)]) for h in range(4)]
        lane = lax.broadcasted_iota(jnp.int32, (1, BLK), 1)
        span_nt = BLK * span_blocks[0].astype(jnp.float32)

        for b in range(4):
            rows = slice(b * 128, b * 128 + 128)
            codes = head_codes[rows]
            table = chosen(codes, pair_rows)
            place = lax.broadcasted_iota(jnp.int32, (128, BLK), 0) + rows.start
            across = lax.broadcasted_iota(jnp.int32, (128, BLK), 1)
            span = span_nt + (across - place).astype(jnp.float32)
            penalty = jnp.sqrt(64.0 * BLK / span)
            factor[rows, :] = factor[rows, :] * table * penalty / partition[0]
            allowed = chosen(lane // 128, [pair_mask[b, n].astype(jnp.float32) for n in range(4)])
            allowed = allowed * (1.0 / BLK)
            right_weight[rows, :] = jnp.broadcast_to(allowed * tail_weight, (128, BLK))
            left_weight[rows, :] = allowed * chosen(codes, weights)

        def left_arrival(slot, n):
            return pltpu.make_async_remote_copy(
                src_ref=left_code.at[left_rows(n)],
                dst_ref=left_in.at[slot, left_rows(n)],
                send_sem=left_send.at[n],
                recv_sem=left_recv.at[slot, n],
                device_id=at_row(sibling),
                device_id_type=MESH,
            )

        def arrive(slot, n):
            right_arrival(slot, n).wait_recv()
            return decode(right_in[slot, right_rows(n), :])

        def half_way(m, carry):
            for slot, n in ((0, m), (1, RIGHT_CHUNKS - 1 - m)):
                right[right_rows(n), :] = arrive(slot, n)
            return carry

        def finish(m, carry):
            for slot, n in ((0, m), (1, RIGHT_CHUNKS - 1 - m)):
                rows = right_rows(n)
                right_sum = right[rows, :] + arrive(slot, n)
                diag = right_sum * right_weight[rows, :] + left[rows, :]
                outside_out[rows, :] = diag
                prob_out[rows, :] = diag * factor[rows, :]
            return carry

        def left_add(n, carry):
            rows = left_rows(n)
            total = jnp.where(counts(row), left[rows, :], 0.0)
            for slot in range(4):
                there = lax.rem(row - core + 2 * slot, ROWS)
                some = counts(sibling) if slot == 0 else counts(there) | counts(there + 1)
                left_arrival(slot, n).wait_recv()
                total = total + jnp.where(some, decode(left_in[slot, rows, :]), 0.0)
            left[rows, :] = total * left_weight[rows, :]
            return carry


        def add_straight(n, carry):
            right[right_rows(n), :] += arrive(2, n)
            return carry

        lax.fori_loop(0, RIGHT_CHUNKS // 2, half_way, 0)
        lax.fori_loop(0, jnp.where(wraps, RIGHT_CHUNKS, 0), add_straight, 0)
        lax.fori_loop(0, LEFT_CHUNKS, left_add, 0)
        lax.fori_loop(RIGHT_CHUNKS // 2, RIGHT_CHUNKS, finish, 0)

    def sent(n, carry):
        right_copy(n).wait_send()
        return carry

    lax.fori_loop(0, RIGHT_CHUNKS, sent, 0)

    @pl.when(jnp.logical_not(is_owner))
    def _():
        def given(n, carry):
            share_copy(n).wait_send()
            return carry

        first = jnp.where(at_owner_chip, 0, (1 - core) * HALF_CHUNKS)
        last = jnp.where(at_owner_chip, LEFT_CHUNKS, (2 - core) * HALF_CHUNKS)
        lax.fori_loop(first, last, given, 0)

    @pl.when(jnp.logical_not(at_owner_chip))
    def _():
        def handed_over(n, carry):
            left_copy(n).wait_send()
            return carry

        lax.fori_loop(core * HALF_CHUNKS, (core + 1) * HALF_CHUNKS, handed_over, 0)


def put_out(diag, prob, outside_out, prob_out, sem):
    copies = [
        pltpu.make_async_copy(src, dst, sem.at[n])
        for n, (src, dst) in enumerate(((diag, outside_out), (prob, prob_out)))
    ]
    for copy in copies:
        copy.start()
    for copy in copies:
        copy.wait()


def per_device(*args):
    vmem = pl.BlockSpec(memory_space=pltpu.VMEM)
    smem = pl.BlockSpec(memory_space=pltpu.SMEM)
    hbm = pl.BlockSpec(memory_space=pltpu.HBM)
    tile = pltpu.VMEM((BLK, BLK), jnp.float32)
    results = pl.pallas_call(
        kernel,
        out_shape=(tile, tile),
        in_specs=[hbm] * 9 + [smem] * 2,
        out_specs=(vmem, vmem),
        scratch_shapes=[
            pltpu.VMEM((BLK, BLK), jnp.bfloat16),
            pltpu.VMEM((BLK, BLK), jnp.bfloat16),
            pltpu.VMEM((BLK, BLK), jnp.bfloat16),
            pltpu.VMEM((BLK, BLK), jnp.float32),
            pltpu.VMEM((BLK, BLK), jnp.float32),
            pltpu.VMEM((BLK, BLK), jnp.float32),
            pltpu.VMEM((1, BLK), jnp.int32),
            pltpu.VMEM((1, BLK), jnp.int32),
            pltpu.SMEM((4, 4), jnp.int32),
            pltpu.SMEM((4,), jnp.float32),
            pltpu.SMEM((4, 4), jnp.float32),
            pltpu.VMEM((BLK, BLK), jnp.float32),
            pltpu.VMEM((BLK, BLK), jnp.float32),
            pltpu.VMEM((BLK, BLK), jnp.int16),
            pltpu.VMEM((BLK, BLK), jnp.int16),
            pltpu.VMEM((3, BLK, BLK), jnp.int16),
            pltpu.VMEM((4, BLK, BLK), jnp.int16),
            pltpu.SemaphoreType.DMA((11,)),
            pltpu.SemaphoreType.DMA((RIGHT_CHUNKS,)),
            pltpu.SemaphoreType.DMA((3, RIGHT_CHUNKS)),
            pltpu.SemaphoreType.DMA((LEFT_CHUNKS,)),
            pltpu.SemaphoreType.DMA((LEFT_CHUNKS,)),
            pltpu.SemaphoreType.DMA((4, LEFT_CHUNKS)),
            pltpu.SemaphoreType.REGULAR,
            pltpu.SemaphoreType.REGULAR,
        ],
        compiler_params=pltpu.CompilerParams(
            collective_id=0, has_side_effects=True, vmem_limit_bytes=62400 * 1024
        ),
        name="outside_window",
    )(*args)
    tile = jax.ShapeDtypeStruct((BLK, BLK), jnp.float32)
    return pl.pallas_call(
        put_out,
        out_shape=(tile, tile),
        in_specs=[vmem] * 2,
        out_specs=(hbm, hbm),
        scratch_shapes=[pltpu.SemaphoreType.DMA((2,))],
        compiler_params=pltpu.CompilerParams(vmem_limit_bytes=1024 * 1024),
        name="put_out",
    )(*results)


def solution(mesh):
    placed = (P("row", "col"),) * 3 + (P(None, "col"),) * 4 + (P(),) * 4
    return jax.shard_map(
        per_device,
        mesh=mesh,
        in_specs=placed,
        out_specs=(P("row", "col"), P("row", "col")),
        check_vma=False,
    )
```

```python
import functools
import math

import jax
import jax.numpy as jnp
from jax import lax
from jax.experimental import pallas as pl
from jax.experimental.pallas import tpu as pltpu
from jax.sharding import PartitionSpec as P

MESH = pl.DeviceIdType.MESH
BLK = 512
ROWS = 8
COLS = 32
RIGHT_CHUNK = 32
RIGHT_CHUNKS = BLK // RIGHT_CHUNK
SHORT = 5
LEFT_CHUNK = 64
LEFT_CHUNKS = BLK // LEFT_CHUNK
HALF_CHUNKS = LEFT_CHUNKS // 2

LOG_LOW = math.log(BLK * 0.0099**2) - 0.01
LOG_HIGH = math.log(5 * BLK * 17.5**2) + 0.01
LOG_MIDDLE = (LOG_LOW + LOG_HIGH) / 2
LOG_STEP = (LOG_HIGH - LOG_LOW) / 65534


def encode(x):
    code = jnp.round((jnp.log(x) - LOG_MIDDLE) * (1.0 / LOG_STEP))
    return jnp.clip(code, -32767.0, 32767.0).astype(jnp.int32).astype(jnp.int16)


def decode(code):
    return jnp.exp(code.astype(jnp.int32).astype(jnp.float32) * LOG_STEP + LOG_MIDDLE)


def kernel(
    outside,
    inside_head,
    inside_tail,
    inside_pair,
    seq_head_any,
    seq_tail_any,
    pair_mask_any,
    split_weight_any,
    pair_weight_any,
    span_blocks,
    partition,
    outside_out,
    prob_out,
    out_tile,
    head_tile,
    tail_tile,
    factor,
    right_weight,
    left_weight,
    seq_head,
    seq_tail,
    pair_mask,
    split_weight,
    pair_weight,
    right,
    left,
    right_code,
    left_code,
    right_in,
    left_in,
    load_sem,
    right_send,
    right_recv,
    share_send,
    left_send,
    left_recv,
    left_ready,
    chain_ready,
):
    row = lax.axis_index("row")
    col = lax.axis_index("col")
    core = lax.rem(row, 2)
    along = lax.rem(col - 2 * (row // 2) + 32, 8)
    reach = lax.rem(col - row + 31, 8) + 1
    is_owner = reach == 8
    owner_row = lax.rem(col, 8)
    chip_away = lax.rem(row // 2 - owner_row // 2 + 4, 4)
    at_owner_chip = chip_away == 0
    sibling = row + 1 - 2 * core
    early = owner_row < 4
    chip_row = row // 2
    waits = (owner_row == 0) & (chip_row >= 2)
    tells = ((chip_row == 2) & (along == 3)) | ((chip_row == 3) & is_owner)
    told_col = jnp.where(is_owner, col + 2 - core, col + 1)

    def at_col(c):
        return (row, lax.rem(c + COLS, COLS))

    def at_row(r):
        return (lax.rem(r + ROWS, ROWS), col)

    upward = (along >= 5) | (along == 0)
    depth = jnp.where(upward, 9 - along, along)
    toward = jnp.where(upward, col + 1, col - 1)
    behind = jnp.where(upward, col - 1, col + 1)
    first_tile, second_tile, third_tile = depth == 2, depth == 3, depth == 4
    beside = along <= 1
    beside_col = jnp.where(along == 0, col - 1, jnp.where(core == 0, col + 1, col - 7))
    wraps = row < 2
    lower = (core == 0) & (row >= 2)
    straight = (wraps & (along == 0)) | (lower & (along == 1))
    joined = first_tile & jnp.logical_not((wraps & (along == 7)) | (lower & (along == 2)))
    takes_straight = wraps | lower
    beside_col = jnp.where(straight, col - reach, beside_col)
    next_col = jnp.where(beside, beside_col, jnp.where(first_tile, col - reach, toward))
    next_slot = jnp.where(straight, 2, jnp.where(beside | (first_tile & upward), 1, 0))

    loads = [
        pltpu.make_async_copy(src, dst, load_sem.at[n])
        for n, (src, dst) in enumerate(
            ((outside, out_tile), (inside_tail, tail_tile), (inside_head, head_tile))
        )
    ]
    for load in loads:
        load.start()

    barrier = pltpu.get_barrier_semaphore()

    def announce(device):
        pl.semaphore_signal(barrier, inc=1, device_id=device, device_id_type=MESH)

    @pl.when((first_tile | second_tile | third_tile) & jnp.logical_not(tells))
    def _():
        announce(at_col(behind))

    @pl.when(waits)
    def _():
        announce(at_col(next_col))

    @pl.when(is_owner & takes_straight)
    def _():
        announce(at_col(jnp.where(wraps, col + 8 - core, col + 1)))

    @pl.when(joined)
    def _():
        announce(at_col(jnp.where(along == 7, col + 1, jnp.where(core == 0, col - 1, col + 7))))

    @pl.when(is_owner)
    def _():
        announce(at_col(col + 7 - core))

    @pl.when(is_owner & jnp.logical_not(tells))
    def _():
        announce(at_col(col + 2 - core))

    @pl.when(jnp.logical_not(at_owner_chip & jnp.logical_not(is_owner)))
    def _():
        announce(at_row(sibling))

    @pl.when(jnp.logical_not(at_owner_chip | early))
    def _():
        announce(at_row(owner_row))

    @pl.when(is_owner & early)
    def _():
        for away in range(2, ROWS):
            announce(at_row(row - core + away))

    loads[0].wait()
    loads[1].wait()

    right[...] = lax.dot_general(
        out_tile[...],
        tail_tile[...],
        (((1,), (1,)), ((), ())),
        preferred_element_type=jnp.float32,
    )

    others = jnp.where(third_tile, 3, 2) + jnp.where(early & jnp.logical_not(at_owner_chip), 1, 0)
    arrivals = jnp.where(is_owner, jnp.where(early, 1, ROWS - 1), others)
    pl.semaphore_wait(barrier, arrivals + jnp.where(tells, 1, 0) - jnp.where(waits, 1, 0))

    @pl.when(tells)
    def _():
        pl.semaphore_signal(chain_ready, inc=1, device_id=at_col(told_col), device_id_type=MESH)

    @pl.when(is_owner & jnp.logical_not(early))
    def _():
        for away in range(2, ROWS):
            pl.semaphore_signal(
                left_ready, inc=1, device_id=at_row(row - core + away), device_id_type=MESH
            )

    def right_rows(n):
        return pl.ds(pl.multiple_of(n * RIGHT_CHUNK, RIGHT_CHUNK), RIGHT_CHUNK)

    def right_copy(n):
        return pltpu.make_async_remote_copy(
            src_ref=right_code.at[right_rows(n)],
            dst_ref=right_in.at[next_slot, right_rows(n)],
            send_sem=right_send.at[n],
            recv_sem=right_recv.at[next_slot, n],
            device_id=at_col(next_col),
            device_id_type=MESH,
        )

    def across_copy(n):
        return pltpu.make_async_remote_copy(
            src_ref=right_code.at[right_rows(n)],
            dst_ref=right_in.at[0, right_rows(n)],
            send_sem=right_send.at[n],
            recv_sem=right_recv.at[0, n],
            device_id=at_col(behind),
            device_id_type=MESH,
        )

    def right_arrival(slot, n):
        return pltpu.make_async_remote_copy(
            src_ref=right_code.at[right_rows(n)],
            dst_ref=right_in.at[slot, right_rows(n)],
            send_sem=right_send.at[n],
            recv_sem=right_recv.at[slot, n],
            device_id=at_col(next_col),
            device_id_type=MESH,
        )

    def chunk(m):
        return jnp.where(upward, RIGHT_CHUNKS - 1 - m, m)

    def send_across(m, carry):
        n = chunk(SHORT - 1 - m)
        right_code[right_rows(n), :] = encode(right[right_rows(n), :])
        across_copy(n).start()
        return carry

    def send_own(m, carry):
        n = chunk(m)
        right_code[right_rows(n), :] = encode(right[right_rows(n), :])
        right_copy(n).start()
        return carry

    def counts(r):
        return col >= lax.rem(col - r + 31, 8) + 1

    def left_rows(n):
        return pl.ds(pl.multiple_of(n * LEFT_CHUNK, LEFT_CHUNK), LEFT_CHUNK)

    def share_copy(n):
        return pltpu.make_async_remote_copy(
            src_ref=left_code.at[left_rows(n)],
            dst_ref=left_in.at[0, left_rows(n)],
            send_sem=share_send.at[n],
            recv_sem=left_recv.at[0, n],
            device_id=at_row(sibling),
            device_id_type=MESH,
        )

    def left_copy(n):
        return pltpu.make_async_remote_copy(
            src_ref=left_code.at[left_rows(n)],
            dst_ref=left_in.at[chip_away, left_rows(n)],
            send_sem=left_send.at[n],
            recv_sem=left_recv.at[chip_away, n],
            device_id=at_row(owner_row),
            device_id_type=MESH,
        )

    def left_part():
        loads[2].wait()

        left[...] = lax.dot_general(
            head_tile[...],
            out_tile[...],
            (((0,), (0,)), ((), ())),
            preferred_element_type=jnp.float32,
        )

        @pl.when(jnp.logical_not(is_owner))
        def _():
            def give(n, carry):
                left_code[left_rows(n), :] = encode(left[left_rows(n), :])
                share_copy(n).start()
                return carry

            first = jnp.where(at_owner_chip, 0, (1 - core) * HALF_CHUNKS)
            last = jnp.where(at_owner_chip, LEFT_CHUNKS, (2 - core) * HALF_CHUNKS)
            lax.fori_loop(first, last, give, 0)

        @pl.when(jnp.logical_not(at_owner_chip))
        def _():
            mine, theirs = counts(row), counts(sibling)

            @pl.when(jnp.logical_not(early))
            def _():
                pl.semaphore_wait(left_ready, 1)


            def merge(n, carry):
                rows = left_rows(n)
                share_copy(n).wait_recv()
                total = jnp.where(mine, left[rows, :], 0.0)
                total = total + jnp.where(theirs, decode(left_in[0, rows, :]), 0.0)
                left_code[rows, :] = encode(jnp.where(mine | theirs, total, 1.0))
                left_copy(n).start()
                return carry

            lax.fori_loop(core * HALF_CHUNKS, (core + 1) * HALF_CHUNKS, merge, 0)

    @pl.when(waits)
    def _():
        left_part()
        pl.semaphore_wait(chain_ready, 1)

    @pl.when(third_tile)
    def _():
        lax.fori_loop(0, SHORT, send_across, 0)

    own_from = jnp.where(third_tile, SHORT, 0)
    own_to = jnp.where(
        first_tile,
        0,
        jnp.where(
            second_tile, SHORT, jnp.where(third_tile, RIGHT_CHUNKS - SHORT, RIGHT_CHUNKS)
        ),
    )
    lax.fori_loop(own_from, own_to, send_own, 0)

    @pl.when(jnp.logical_not(waits))
    def _():
        left_part()

    def pass_on(m, carry):
        n = chunk(m)
        rows = right_rows(n)
        right_arrival(0, n).wait_recv()
        right_code[rows, :] = encode(right[rows, :] + decode(right_in[0, rows, :]))
        right_copy(n).start()
        return carry

    def pass_on_both(m, carry):
        n = chunk(m)
        rows = right_rows(n)
        right_arrival(1, n).wait_recv()
        total = right[rows, :] + decode(right_in[1, rows, :])
        right_arrival(0, n).wait_recv()
        right_code[rows, :] = encode(total + decode(right_in[0, rows, :]))
        right_copy(n).start()
        return carry

    @pl.when(joined)
    def _():
        lax.fori_loop(0, RIGHT_CHUNKS, pass_on_both, 0)

    @pl.when(jnp.logical_not(joined | beside))
    def _():
        lax.fori_loop(own_to, RIGHT_CHUNKS, pass_on, 0)

    @pl.when(jnp.logical_not(is_owner))
    def _():
        outside_out[...] = jnp.zeros((BLK, BLK), jnp.float32)
        prob_out[...] = jnp.zeros((BLK, BLK), jnp.float32)

    @pl.when(is_owner)
    def _():
        owner_loads = [
            pltpu.make_async_copy(src, dst, load_sem.at[3 + n])
            for n, (src, dst) in enumerate(
                (
                    (inside_pair, factor),
                    (seq_head_any, seq_head),
                    (seq_tail_any, seq_tail),
                    (pair_mask_any, pair_mask),
                    (split_weight_any, split_weight),
                    (pair_weight_any, pair_weight),
                )
            )
        ]
        for load in owner_loads:
            load.start()
        for load in owner_loads:
            load.wait()
        head_codes = jnp.transpose(
            jnp.broadcast_to(seq_head[...].astype(jnp.float32), (8, BLK)), (1, 0)
        )[:, :1]
        tail_codes = seq_tail[...]

        def chosen(codes, values):
            picked = jnp.where(codes == 1, values[1], values[0])
            picked = jnp.where(codes == 2, values[2], picked)
            return jnp.where(codes == 3, values[3], picked)

        weights = [split_weight[n] for n in range(4)]
        tail_weight = chosen(tail_codes, weights)
        pair_rows = [chosen(tail_codes, [pair_weight[h, t] for t in range(4)]) for h in range(4)]
        lane = lax.broadcasted_iota(jnp.int32, (1, BLK), 1)
        span_nt = BLK * span_blocks[0].astype(jnp.float32)

        for b in range(4):
            rows = slice(b * 128, b * 128 + 128)
            codes = head_codes[rows]
            table = chosen(codes, pair_rows)
            place = lax.broadcasted_iota(jnp.int32, (128, BLK), 0) + rows.start
            across = lax.broadcasted_iota(jnp.int32, (128, BLK), 1)
            span = span_nt + (across - place).astype(jnp.float32)
            penalty = jnp.sqrt(64.0 * BLK / span)
            factor[rows, :] = factor[rows, :] * table * penalty / partition[0]
            allowed = chosen(lane // 128, [pair_mask[b, n].astype(jnp.float32) for n in range(4)])
            allowed = allowed * (1.0 / BLK)
            right_weight[rows, :] = jnp.broadcast_to(allowed * tail_weight, (128, BLK))
            left_weight[rows, :] = allowed * chosen(codes, weights)

        def left_arrival(slot, n):
            return pltpu.make_async_remote_copy(
                src_ref=left_code.at[left_rows(n)],
                dst_ref=left_in.at[slot, left_rows(n)],
                send_sem=left_send.at[n],
                recv_sem=left_recv.at[slot, n],
                device_id=at_row(sibling),
                device_id_type=MESH,
            )

        def arrive(slot, n):
            right_arrival(slot, n).wait_recv()
            return decode(right_in[slot, right_rows(n), :])

        def half_way(m, carry):
            for slot, n in ((0, m), (1, RIGHT_CHUNKS - 1 - m)):
                right[right_rows(n), :] = arrive(slot, n)
            return carry

        def finish(m, carry):
            for slot, n in ((0, m), (1, RIGHT_CHUNKS - 1 - m)):
                rows = right_rows(n)
                right_sum = right[rows, :] + arrive(slot, n)
                diag = right_sum * right_weight[rows, :] + left[rows, :]
                outside_out[rows, :] = diag
                prob_out[rows, :] = diag * factor[rows, :]
            return carry

        def left_add(n, carry):
            rows = left_rows(n)
            total = jnp.where(counts(row), left[rows, :], 0.0)
            for slot in range(4):
                there = lax.rem(row - core + 2 * slot, ROWS)
                some = counts(sibling) if slot == 0 else counts(there) | counts(there + 1)
                left_arrival(slot, n).wait_recv()
                total = total + jnp.where(some, decode(left_in[slot, rows, :]), 0.0)
            left[rows, :] = total * left_weight[rows, :]
            return carry


        def add_straight(n, carry):
            right[right_rows(n), :] += arrive(2, n)
            return carry

        lax.fori_loop(0, RIGHT_CHUNKS // 2, half_way, 0)
        lax.fori_loop(0, jnp.where(takes_straight, RIGHT_CHUNKS, 0), add_straight, 0)
        lax.fori_loop(0, LEFT_CHUNKS, left_add, 0)
        lax.fori_loop(RIGHT_CHUNKS // 2, RIGHT_CHUNKS, finish, 0)

    def sent(n, carry):
        right_copy(n).wait_send()
        return carry

    lax.fori_loop(0, RIGHT_CHUNKS, sent, 0)

    @pl.when(jnp.logical_not(is_owner))
    def _():
        def given(n, carry):
            share_copy(n).wait_send()
            return carry

        first = jnp.where(at_owner_chip, 0, (1 - core) * HALF_CHUNKS)
        last = jnp.where(at_owner_chip, LEFT_CHUNKS, (2 - core) * HALF_CHUNKS)
        lax.fori_loop(first, last, given, 0)

    @pl.when(jnp.logical_not(at_owner_chip))
    def _():
        def handed_over(n, carry):
            left_copy(n).wait_send()
            return carry

        lax.fori_loop(core * HALF_CHUNKS, (core + 1) * HALF_CHUNKS, handed_over, 0)


def put_out(diag, prob, outside_out, prob_out, sem):
    copies = [
        pltpu.make_async_copy(src, dst, sem.at[n])
        for n, (src, dst) in enumerate(((diag, outside_out), (prob, prob_out)))
    ]
    for copy in copies:
        copy.start()
    for copy in copies:
        copy.wait()


def per_device(*args):
    vmem = pl.BlockSpec(memory_space=pltpu.VMEM)
    smem = pl.BlockSpec(memory_space=pltpu.SMEM)
    hbm = pl.BlockSpec(memory_space=pltpu.HBM)
    tile = pltpu.VMEM((BLK, BLK), jnp.float32)
    results = pl.pallas_call(
        kernel,
        out_shape=(tile, tile),
        in_specs=[hbm] * 9 + [smem] * 2,
        out_specs=(vmem, vmem),
        scratch_shapes=[
            pltpu.VMEM((BLK, BLK), jnp.bfloat16),
            pltpu.VMEM((BLK, BLK), jnp.bfloat16),
            pltpu.VMEM((BLK, BLK), jnp.bfloat16),
            pltpu.VMEM((BLK, BLK), jnp.float32),
            pltpu.VMEM((BLK, BLK), jnp.float32),
            pltpu.VMEM((BLK, BLK), jnp.float32),
            pltpu.VMEM((1, BLK), jnp.int32),
            pltpu.VMEM((1, BLK), jnp.int32),
            pltpu.SMEM((4, 4), jnp.int32),
            pltpu.SMEM((4,), jnp.float32),
            pltpu.SMEM((4, 4), jnp.float32),
            pltpu.VMEM((BLK, BLK), jnp.float32),
            pltpu.VMEM((BLK, BLK), jnp.float32),
            pltpu.VMEM((BLK, BLK), jnp.int16),
            pltpu.VMEM((BLK, BLK), jnp.int16),
            pltpu.VMEM((3, BLK, BLK), jnp.int16),
            pltpu.VMEM((4, BLK, BLK), jnp.int16),
            pltpu.SemaphoreType.DMA((11,)),
            pltpu.SemaphoreType.DMA((RIGHT_CHUNKS,)),
            pltpu.SemaphoreType.DMA((3, RIGHT_CHUNKS)),
            pltpu.SemaphoreType.DMA((LEFT_CHUNKS,)),
            pltpu.SemaphoreType.DMA((LEFT_CHUNKS,)),
            pltpu.SemaphoreType.DMA((4, LEFT_CHUNKS)),
            pltpu.SemaphoreType.REGULAR,
            pltpu.SemaphoreType.REGULAR,
        ],
        compiler_params=pltpu.CompilerParams(
            collective_id=0, has_side_effects=True, vmem_limit_bytes=62400 * 1024
        ),
        name="outside_window",
    )(*args)
    tile = jax.ShapeDtypeStruct((BLK, BLK), jnp.float32)
    return pl.pallas_call(
        put_out,
        out_shape=(tile, tile),
        in_specs=[vmem] * 2,
        out_specs=(hbm, hbm),
        scratch_shapes=[pltpu.SemaphoreType.DMA((2,))],
        compiler_params=pltpu.CompilerParams(vmem_limit_bytes=1024 * 1024),
        name="put_out",
    )(*results)


def solution(mesh):
    placed = (P("row", "col"),) * 3 + (P(None, "col"),) * 4 + (P(),) * 4
    return jax.shard_map(
        per_device,
        mesh=mesh,
        in_specs=placed,
        out_specs=(P("row", "col"), P("row", "col")),
        check_vma=False,
    )
```

```python
import functools
import math

import jax
import jax.numpy as jnp
from jax import lax
from jax.experimental import pallas as pl
from jax.experimental.pallas import tpu as pltpu
from jax.sharding import PartitionSpec as P

MESH = pl.DeviceIdType.MESH
BLK = 512
ROWS = 8
COLS = 32
RIGHT_CHUNK = 32
RIGHT_CHUNKS = BLK // RIGHT_CHUNK
SHORT = 5
LEFT_CHUNK = 128
LEFT_CHUNKS = BLK // LEFT_CHUNK
HALF_CHUNKS = LEFT_CHUNKS // 2

LOG_LOW = math.log(BLK * 0.0099**2) - 0.01
LOG_HIGH = math.log(5 * BLK * 17.5**2) + 0.01
LOG_MIDDLE = (LOG_LOW + LOG_HIGH) / 2
LOG_STEP = (LOG_HIGH - LOG_LOW) / 65534


def encode(x):
    code = jnp.round((jnp.log(x) - LOG_MIDDLE) * (1.0 / LOG_STEP))
    return jnp.clip(code, -32767.0, 32767.0).astype(jnp.int32).astype(jnp.int16)


def decode(code):
    return jnp.exp(code.astype(jnp.int32).astype(jnp.float32) * LOG_STEP + LOG_MIDDLE)


def kernel(
    outside,
    inside_head,
    inside_tail,
    inside_pair,
    seq_head_any,
    seq_tail_any,
    pair_mask_any,
    split_weight_any,
    pair_weight_any,
    span_blocks,
    partition,
    outside_out,
    prob_out,
    out_tile,
    head_tile,
    tail_tile,
    factor,
    right_weight,
    left_weight,
    seq_head,
    seq_tail,
    pair_mask,
    split_weight,
    pair_weight,
    right,
    left,
    right_code,
    left_code,
    right_in,
    left_in,
    load_sem,
    right_send,
    right_recv,
    share_send,
    left_send,
    left_recv,
    left_ready,
    chain_ready,
):
    row = lax.axis_index("row")
    col = lax.axis_index("col")
    core = lax.rem(row, 2)
    along = lax.rem(col - 2 * (row // 2) + 32, 8)
    reach = lax.rem(col - row + 31, 8) + 1
    is_owner = reach == 8
    owner_row = lax.rem(col, 8)
    chip_away = lax.rem(row // 2 - owner_row // 2 + 4, 4)
    at_owner_chip = chip_away == 0
    sibling = row + 1 - 2 * core
    early = owner_row < 4
    chip_row = row // 2
    waits = (owner_row == 0) & (chip_row >= 2)
    tells = ((chip_row == 2) & (along == 3)) | ((chip_row == 3) & is_owner)
    told_col = jnp.where(is_owner, col + 2 - core, col + 1)

    def at_col(c):
        return (row, lax.rem(c + COLS, COLS))

    def at_row(r):
        return (lax.rem(r + ROWS, ROWS), col)

    upward = (along >= 5) | (along == 0)
    depth = jnp.where(upward, 9 - along, along)
    toward = jnp.where(upward, col + 1, col - 1)
    behind = jnp.where(upward, col - 1, col + 1)
    first_tile, second_tile, third_tile = depth == 2, depth == 3, depth == 4
    beside = along <= 1
    beside_col = jnp.where(along == 0, col - 1, jnp.where(core == 0, col + 1, col - 7))
    wraps = row < 2
    lower = (core == 0) & (row >= 2)
    straight = (wraps & (along == 0)) | (lower & (along == 1))
    joined = first_tile & jnp.logical_not((wraps & (along == 7)) | (lower & (along == 2)))
    takes_straight = wraps | lower
    beside_col = jnp.where(straight, col - reach, beside_col)
    next_col = jnp.where(beside, beside_col, jnp.where(first_tile, col - reach, toward))
    next_slot = jnp.where(straight, 2, jnp.where(beside | (first_tile & upward), 1, 0))

    loads = [
        pltpu.make_async_copy(src, dst, load_sem.at[n])
        for n, (src, dst) in enumerate(
            ((outside, out_tile), (inside_tail, tail_tile), (inside_head, head_tile))
        )
    ]
    for load in loads:
        load.start()

    barrier = pltpu.get_barrier_semaphore()

    def announce(device):
        pl.semaphore_signal(barrier, inc=1, device_id=device, device_id_type=MESH)

    @pl.when((first_tile | second_tile | third_tile) & jnp.logical_not(tells))
    def _():
        announce(at_col(behind))

    @pl.when(waits)
    def _():
        announce(at_col(next_col))

    @pl.when(is_owner & takes_straight)
    def _():
        announce(at_col(jnp.where(wraps, col + 8 - core, col + 1)))

    @pl.when(joined)
    def _():
        announce(at_col(jnp.where(along == 7, col + 1, jnp.where(core == 0, col - 1, col + 7))))

    @pl.when(is_owner)
    def _():
        announce(at_col(col + 7 - core))

    @pl.when(is_owner & jnp.logical_not(tells))
    def _():
        announce(at_col(col + 2 - core))

    @pl.when(jnp.logical_not(at_owner_chip & jnp.logical_not(is_owner)))
    def _():
        announce(at_row(sibling))

    @pl.when(jnp.logical_not(at_owner_chip | early))
    def _():
        announce(at_row(owner_row))

    @pl.when(is_owner & early)
    def _():
        for away in range(2, ROWS):
            announce(at_row(row - core + away))

    loads[0].wait()
    loads[1].wait()

    right[...] = lax.dot_general(
        out_tile[...],
        tail_tile[...],
        (((1,), (1,)), ((), ())),
        preferred_element_type=jnp.float32,
    )

    others = jnp.where(third_tile, 3, 2) + jnp.where(early & jnp.logical_not(at_owner_chip), 1, 0)
    arrivals = jnp.where(is_owner, jnp.where(early, 1, ROWS - 1), others)
    pl.semaphore_wait(barrier, arrivals + jnp.where(tells, 1, 0) - jnp.where(waits, 1, 0))

    @pl.when(tells)
    def _():
        pl.semaphore_signal(chain_ready, inc=1, device_id=at_col(told_col), device_id_type=MESH)

    @pl.when(is_owner & jnp.logical_not(early))
    def _():
        for away in range(2, ROWS):
            pl.semaphore_signal(
                left_ready, inc=1, device_id=at_row(row - core + away), device_id_type=MESH
            )

    def right_rows(n):
        return pl.ds(pl.multiple_of(n * RIGHT_CHUNK, RIGHT_CHUNK), RIGHT_CHUNK)

    def right_copy(n):
        return pltpu.make_async_remote_copy(
            src_ref=right_code.at[right_rows(n)],
            dst_ref=right_in.at[next_slot, right_rows(n)],
            send_sem=right_send.at[n],
            recv_sem=right_recv.at[next_slot, n],
            device_id=at_col(next_col),
            device_id_type=MESH,
        )

    def across_copy(n):
        return pltpu.make_async_remote_copy(
            src_ref=right_code.at[right_rows(n)],
            dst_ref=right_in.at[0, right_rows(n)],
            send_sem=right_send.at[n],
            recv_sem=right_recv.at[0, n],
            device_id=at_col(behind),
            device_id_type=MESH,
        )

    def right_arrival(slot, n):
        return pltpu.make_async_remote_copy(
            src_ref=right_code.at[right_rows(n)],
            dst_ref=right_in.at[slot, right_rows(n)],
            send_sem=right_send.at[n],
            recv_sem=right_recv.at[slot, n],
            device_id=at_col(next_col),
            device_id_type=MESH,
        )

    def chunk(m):
        return jnp.where(upward, RIGHT_CHUNKS - 1 - m, m)

    def send_across(m, carry):
        n = chunk(SHORT - 1 - m)
        right_code[right_rows(n), :] = encode(right[right_rows(n), :])
        across_copy(n).start()
        return carry

    def send_own(m, carry):
        n = chunk(m)
        right_code[right_rows(n), :] = encode(right[right_rows(n), :])
        right_copy(n).start()
        return carry

    def counts(r):
        return col >= lax.rem(col - r + 31, 8) + 1

    def left_rows(n):
        return pl.ds(pl.multiple_of(n * LEFT_CHUNK, LEFT_CHUNK), LEFT_CHUNK)

    def share_copy(n):
        return pltpu.make_async_remote_copy(
            src_ref=left_code.at[left_rows(n)],
            dst_ref=left_in.at[0, left_rows(n)],
            send_sem=share_send.at[n],
            recv_sem=left_recv.at[0, n],
            device_id=at_row(sibling),
            device_id_type=MESH,
        )

    def left_copy(n):
        return pltpu.make_async_remote_copy(
            src_ref=left_code.at[left_rows(n)],
            dst_ref=left_in.at[chip_away, left_rows(n)],
            send_sem=left_send.at[n],
            recv_sem=left_recv.at[chip_away, n],
            device_id=at_row(owner_row),
            device_id_type=MESH,
        )

    def left_part():
        loads[2].wait()

        left[...] = lax.dot_general(
            head_tile[...],
            out_tile[...],
            (((0,), (0,)), ((), ())),
            preferred_element_type=jnp.float32,
        )

        @pl.when(jnp.logical_not(is_owner))
        def _():
            def give(n, carry):
                left_code[left_rows(n), :] = encode(left[left_rows(n), :])
                share_copy(n).start()
                return carry

            first = jnp.where(at_owner_chip, 0, (1 - core) * HALF_CHUNKS)
            last = jnp.where(at_owner_chip, LEFT_CHUNKS, (2 - core) * HALF_CHUNKS)
            lax.fori_loop(first, last, give, 0)

        @pl.when(jnp.logical_not(at_owner_chip))
        def _():
            mine, theirs = counts(row), counts(sibling)

            @pl.when(jnp.logical_not(early))
            def _():
                pl.semaphore_wait(left_ready, 1)


            def merge(n, carry):
                rows = left_rows(n)
                share_copy(n).wait_recv()
                total = jnp.where(mine, left[rows, :], 0.0)
                total = total + jnp.where(theirs, decode(left_in[0, rows, :]), 0.0)
                left_code[rows, :] = encode(jnp.where(mine | theirs, total, 1.0))
                left_copy(n).start()
                return carry

            lax.fori_loop(core * HALF_CHUNKS, (core + 1) * HALF_CHUNKS, merge, 0)

    @pl.when(waits)
    def _():
        left_part()
        pl.semaphore_wait(chain_ready, 1)

    @pl.when(third_tile)
    def _():
        lax.fori_loop(0, SHORT, send_across, 0)

    own_from = jnp.where(third_tile, SHORT, 0)
    own_to = jnp.where(
        first_tile,
        0,
        jnp.where(
            second_tile, SHORT, jnp.where(third_tile, RIGHT_CHUNKS - SHORT, RIGHT_CHUNKS)
        ),
    )
    lax.fori_loop(own_from, own_to, send_own, 0)

    @pl.when(jnp.logical_not(waits))
    def _():
        left_part()

    def pass_on(m, carry):
        n = chunk(m)
        rows = right_rows(n)
        right_arrival(0, n).wait_recv()
        right_code[rows, :] = encode(right[rows, :] + decode(right_in[0, rows, :]))
        right_copy(n).start()
        return carry

    def pass_on_both(m, carry):
        n = chunk(m)
        rows = right_rows(n)
        right_arrival(1, n).wait_recv()
        total = right[rows, :] + decode(right_in[1, rows, :])
        right_arrival(0, n).wait_recv()
        right_code[rows, :] = encode(total + decode(right_in[0, rows, :]))
        right_copy(n).start()
        return carry

    @pl.when(joined)
    def _():
        lax.fori_loop(0, RIGHT_CHUNKS, pass_on_both, 0)

    @pl.when(jnp.logical_not(joined | beside))
    def _():
        lax.fori_loop(own_to, RIGHT_CHUNKS, pass_on, 0)

    @pl.when(jnp.logical_not(is_owner))
    def _():
        outside_out[...] = jnp.zeros((BLK, BLK), jnp.float32)
        prob_out[...] = jnp.zeros((BLK, BLK), jnp.float32)

    @pl.when(is_owner)
    def _():
        owner_loads = [
            pltpu.make_async_copy(src, dst, load_sem.at[3 + n])
            for n, (src, dst) in enumerate(
                (
                    (inside_pair, factor),
                    (seq_head_any, seq_head),
                    (seq_tail_any, seq_tail),
                    (pair_mask_any, pair_mask),
                    (split_weight_any, split_weight),
                    (pair_weight_any, pair_weight),
                )
            )
        ]
        for load in owner_loads:
            load.start()
        for load in owner_loads:
            load.wait()
        head_codes = jnp.transpose(
            jnp.broadcast_to(seq_head[...].astype(jnp.float32), (8, BLK)), (1, 0)
        )[:, :1]
        tail_codes = seq_tail[...]

        def chosen(codes, values):
            picked = jnp.where(codes == 1, values[1], values[0])
            picked = jnp.where(codes == 2, values[2], picked)
            return jnp.where(codes == 3, values[3], picked)

        weights = [split_weight[n] for n in range(4)]
        tail_weight = chosen(tail_codes, weights)
        pair_rows = [chosen(tail_codes, [pair_weight[h, t] for t in range(4)]) for h in range(4)]
        lane = lax.broadcasted_iota(jnp.int32, (1, BLK), 1)
        span_nt = BLK * span_blocks[0].astype(jnp.float32)

        for b in range(4):
            rows = slice(b * 128, b * 128 + 128)
            codes = head_codes[rows]
            table = chosen(codes, pair_rows)
            place = lax.broadcasted_iota(jnp.int32, (128, BLK), 0) + rows.start
            across = lax.broadcasted_iota(jnp.int32, (128, BLK), 1)
            span = span_nt + (across - place).astype(jnp.float32)
            penalty = jnp.sqrt(64.0 * BLK / span)
            factor[rows, :] = factor[rows, :] * table * penalty / partition[0]
            allowed = chosen(lane // 128, [pair_mask[b, n].astype(jnp.float32) for n in range(4)])
            allowed = allowed * (1.0 / BLK)
            right_weight[rows, :] = jnp.broadcast_to(allowed * tail_weight, (128, BLK))
            left_weight[rows, :] = allowed * chosen(codes, weights)

        def left_arrival(slot, n):
            return pltpu.make_async_remote_copy(
                src_ref=left_code.at[left_rows(n)],
                dst_ref=left_in.at[slot, left_rows(n)],
                send_sem=left_send.at[n],
                recv_sem=left_recv.at[slot, n],
                device_id=at_row(sibling),
                device_id_type=MESH,
            )

        def arrive(slot, n):
            right_arrival(slot, n).wait_recv()
            return decode(right_in[slot, right_rows(n), :])

        def half_way(m, carry):
            for slot, n in ((0, m), (1, RIGHT_CHUNKS - 1 - m)):
                right[right_rows(n), :] = arrive(slot, n)
            return carry

        def finish(m, carry):
            for slot, n in ((0, m), (1, RIGHT_CHUNKS - 1 - m)):
                rows = right_rows(n)
                right_sum = right[rows, :] + arrive(slot, n)
                diag = right_sum * right_weight[rows, :] + left[rows, :]
                outside_out[rows, :] = diag
                prob_out[rows, :] = diag * factor[rows, :]
            return carry

        def left_add(n, carry):
            rows = left_rows(n)
            total = jnp.where(counts(row), left[rows, :], 0.0)
            for slot in range(4):
                there = lax.rem(row - core + 2 * slot, ROWS)
                some = counts(sibling) if slot == 0 else counts(there) | counts(there + 1)
                left_arrival(slot, n).wait_recv()
                total = total + jnp.where(some, decode(left_in[slot, rows, :]), 0.0)
            left[rows, :] = total * left_weight[rows, :]
            return carry


        def add_straight(n, carry):
            right[right_rows(n), :] += arrive(2, n)
            return carry

        lax.fori_loop(0, RIGHT_CHUNKS // 2, half_way, 0)
        lax.fori_loop(0, jnp.where(takes_straight, RIGHT_CHUNKS, 0), add_straight, 0)
        lax.fori_loop(0, LEFT_CHUNKS, left_add, 0)
        lax.fori_loop(RIGHT_CHUNKS // 2, RIGHT_CHUNKS, finish, 0)

    def sent(n, carry):
        right_copy(n).wait_send()
        return carry

    lax.fori_loop(0, RIGHT_CHUNKS, sent, 0)

    @pl.when(jnp.logical_not(is_owner))
    def _():
        def given(n, carry):
            share_copy(n).wait_send()
            return carry

        first = jnp.where(at_owner_chip, 0, (1 - core) * HALF_CHUNKS)
        last = jnp.where(at_owner_chip, LEFT_CHUNKS, (2 - core) * HALF_CHUNKS)
        lax.fori_loop(first, last, given, 0)

    @pl.when(jnp.logical_not(at_owner_chip))
    def _():
        def handed_over(n, carry):
            left_copy(n).wait_send()
            return carry

        lax.fori_loop(core * HALF_CHUNKS, (core + 1) * HALF_CHUNKS, handed_over, 0)


def put_out(diag, prob, outside_out, prob_out, sem):
    copies = [
        pltpu.make_async_copy(src, dst, sem.at[n])
        for n, (src, dst) in enumerate(((diag, outside_out), (prob, prob_out)))
    ]
    for copy in copies:
        copy.start()
    for copy in copies:
        copy.wait()


def per_device(*args):
    vmem = pl.BlockSpec(memory_space=pltpu.VMEM)
    smem = pl.BlockSpec(memory_space=pltpu.SMEM)
    hbm = pl.BlockSpec(memory_space=pltpu.HBM)
    tile = pltpu.VMEM((BLK, BLK), jnp.float32)
    results = pl.pallas_call(
        kernel,
        out_shape=(tile, tile),
        in_specs=[hbm] * 9 + [smem] * 2,
        out_specs=(vmem, vmem),
        scratch_shapes=[
            pltpu.VMEM((BLK, BLK), jnp.bfloat16),
            pltpu.VMEM((BLK, BLK), jnp.bfloat16),
            pltpu.VMEM((BLK, BLK), jnp.bfloat16),
            pltpu.VMEM((BLK, BLK), jnp.float32),
            pltpu.VMEM((BLK, BLK), jnp.float32),
            pltpu.VMEM((BLK, BLK), jnp.float32),
            pltpu.VMEM((1, BLK), jnp.int32),
            pltpu.VMEM((1, BLK), jnp.int32),
            pltpu.SMEM((4, 4), jnp.int32),
            pltpu.SMEM((4,), jnp.float32),
            pltpu.SMEM((4, 4), jnp.float32),
            pltpu.VMEM((BLK, BLK), jnp.float32),
            pltpu.VMEM((BLK, BLK), jnp.float32),
            pltpu.VMEM((BLK, BLK), jnp.int16),
            pltpu.VMEM((BLK, BLK), jnp.int16),
            pltpu.VMEM((3, BLK, BLK), jnp.int16),
            pltpu.VMEM((4, BLK, BLK), jnp.int16),
            pltpu.SemaphoreType.DMA((11,)),
            pltpu.SemaphoreType.DMA((RIGHT_CHUNKS,)),
            pltpu.SemaphoreType.DMA((3, RIGHT_CHUNKS)),
            pltpu.SemaphoreType.DMA((LEFT_CHUNKS,)),
            pltpu.SemaphoreType.DMA((LEFT_CHUNKS,)),
            pltpu.SemaphoreType.DMA((4, LEFT_CHUNKS)),
            pltpu.SemaphoreType.REGULAR,
            pltpu.SemaphoreType.REGULAR,
        ],
        compiler_params=pltpu.CompilerParams(
            collective_id=0, has_side_effects=True, vmem_limit_bytes=62400 * 1024
        ),
        name="outside_window",
    )(*args)
    tile = jax.ShapeDtypeStruct((BLK, BLK), jnp.float32)
    return pl.pallas_call(
        put_out,
        out_shape=(tile, tile),
        in_specs=[vmem] * 2,
        out_specs=(hbm, hbm),
        scratch_shapes=[pltpu.SemaphoreType.DMA((2,))],
        compiler_params=pltpu.CompilerParams(vmem_limit_bytes=1024 * 1024),
        name="put_out",
    )(*results)


def solution(mesh):
    placed = (P("row", "col"),) * 3 + (P(None, "col"),) * 4 + (P(),) * 4
    return jax.shard_map(
        per_device,
        mesh=mesh,
        in_specs=placed,
        out_specs=(P("row", "col"), P("row", "col")),
        check_vma=False,
    )
```
